512 devices in a mesh: row: 16 (over x, z_hi, core), col: 32 (over z_lo, y).
Axes of the slice: x: 4, y: 8, z: 8 (z_hi: 2, z_lo: 4; z = z_hi * 4 + z_lo), core: 2. Of those that a mesh axis runs over, the one named last changes fastest.
Arguments:
- block_cols: int32 [512, 16], P(('row', 'col')), may hold values from 0 to 511, as said below
- blocks: bfloat16 [512, 16, 128, 128], P(('row', 'col')), as said below
Outputs:
- purified: bfloat16 [512, 16, 128, 128], P(('row', 'col'))
The draws below stay inside these ranges and needn't reach their ends.
Inputs may be any that keep to these rules, and one draw needn't show every extreme that they name: `block_cols`: block row i lists 16 distinct block columns, all within cyclic distance 8 of i, in increasing order of their offset (j - i) taken in -8 .. 8; block column j is listed in row i exactly when i is listed in row j. `blocks`: the matrix is symmetric: the block listed for (i, j) is the transpose of the block listed for (j, i).
All inputs are finite; a program needn't handle non-finite values.
Results may differ from the reference program's by a relative error of at most 0.0039.
Values may be sent and summed in bfloat16 or wider, within the bound.
A program may use at most 64 MiB of HBM per device.

```python
import jax
import jax.numpy as jnp

B = 128
NNZ = 16
BAND = 8
NB = 512


def pattern_slots(key):
    groups = NB // 16
    partner_bits = jax.random.randint(key, (groups,), 1, 9).astype(jnp.int32)
    row_ids = jnp.arange(NB, dtype=jnp.int32)
    partner = jnp.bitwise_xor(row_ids, jnp.repeat(partner_bits, 16))
    missing = partner - row_ids + BAND
    slot_ids = jnp.arange(NNZ, dtype=jnp.int32)
    slot_index = slot_ids[None, :] + (slot_ids[None, :] >= missing[:, None]).astype(jnp.int32)
    return (row_ids, slot_index)


def draw_block_cols(key, part):
    row_ids, slot_index = pattern_slots(key)
    return ((row_ids[:, None] + slot_index - BAND) % NB).astype(jnp.int32)


def draw_blocks(key, part):
    row_ids, slot_index = pattern_slots(key)
    key = jax.random.fold_in(key, 7)
    random_half = 0.1 * jax.random.normal(key, (NB, BAND + 1, B, B), jnp.float32)
    row_scale = jnp.ones((NB,), jnp.float32)
    pieces = []
    for target in range(2 * BAND + 1):
        if target < BAND:
            distance = BAND - target
            piece = jnp.swapaxes(jnp.roll(random_half[:, distance], distance, axis=0), -1, -2)
        elif target == BAND:
            piece = 0.70710678 * (random_half[:, 0] + jnp.swapaxes(random_half[:, 0], -1, -2))
        else:
            piece = random_half[:, target - BAND]
        partner_scale = jnp.roll(row_scale, -(target - BAND))
        pieces.append(piece * partner_scale[:, None, None])
    banded = jnp.stack(pieces, axis=1)
    values = jnp.take_along_axis(banded, slot_index[:, :, None, None], axis=1)
    return values.astype(jnp.bfloat16)


def setup_inputs(seed: int = 0) -> dict:
    keys = jax.random.split(jax.random.key(seed), 3)
    return {
        "block_cols": draw_block_cols(jax.random.fold_in(keys[2], 71), 0),
        "blocks": draw_blocks(jax.random.fold_in(keys[2], 71), 0),
    }


def expand_rows(blocks, block_cols):
    count = blocks.shape[0]
    row_ids = jnp.arange(count, dtype=jnp.int32)
    offsets = (block_cols - row_ids[:, None] + BAND) % count
    onehot = (offsets[:, :, None] == jnp.arange(2 * BAND + 1, dtype=jnp.int32)[None, None, :]).astype(jnp.float32)
    banded = jnp.einsum("rsb,rsxy->rbxy", onehot, blocks.astype(jnp.float32))
    present = jnp.sum(onehot, axis=1)
    return banded, present, onehot


def band_product(factor, source):
    window = 2 * BAND + 1
    result = jnp.zeros(factor.shape, jnp.float32)
    for offset in range(window):
        shifted = jnp.roll(source, -(offset - BAND), axis=0)
        first_slot = max(0, offset - BAND)
        last_slot = min(window, offset + BAND + 1)
        partial_value = jnp.einsum("rxy,rlyz->rlxz", factor[:, offset], shifted[:, first_slot - offset + BAND:last_slot - offset + BAND])
        result = result.at[:, first_slot:last_slot].add(partial_value)
    return result


def reference(block_cols, blocks):
    banded, present, onehot = expand_rows(blocks, block_cols)
    squared = (band_product(banded, banded) * present[:, :, None, None]).astype(jnp.bfloat16)
    squared_wide = squared.astype(jnp.float32)
    cubic = band_product(squared_wide, banded) * present[:, :, None, None]
    newband = (3.0 * squared_wide - 2.0 * cubic).astype(jnp.bfloat16)
    return jnp.einsum("rsb,rbxy->rsxy", onehot, newband.astype(jnp.float32)).astype(jnp.bfloat16)
```

```python
import functools

import jax
import jax.numpy as jnp
from jax import lax
from jax.experimental import pallas as pl
from jax.experimental.pallas import tpu as pltpu
from jax.sharding import PartitionSpec as P

BAND = 8
WINDOW = 2 * BAND + 1
HALF = BAND + 1
RING = 8
MESH = pl.DeviceIdType.MESH

EVENTS = (
    (1, 16200, 231488, 86344, 12088, 231488, 7976, 223264, 219152),
    (1, 131144, 16200, 16200, 86344, 16200, 231488, 86344, 24352),
    (1, 68426, 131144, 131401, 131658, 131144, 86601, 17485, 86344),
    (1, 221208, 86858, 221208, 221208, 86601, 131915, 132429, 131144),
    (1, 67912, 14144, 86858, 14144, 10032, 16200, 86601, 71952),
    (1, 17485, 86601, 17999, 86601, 86858, 69896, 18256, 28464),
    (1, 131401, 131915, 229432, 227376, 225320, 227376, 227376, 221208),
    (1, 223264, 221208, 132172, 131144, 132172, 131144, 132686, 132943),
    (1, 68169, 17485, 12088, 16200, 12088, 12088, 86858, 30520),
    (1, 17742, 69896, 74008, 87115, 69896, 86344, 17742, 86601),
    (1, 68940, 17999, 14144, 87372, 17485, 86858, 17999, 32576),
    (1, 18256, 71952, 87115, 17742, 71952, 17228, 69896, 86858),
    (1, 131658, 233544, 231488, 229432, 131401, 223264, 231488, 223264),
    (1, 225320, 131401, 131144, 131401, 223264, 131401, 131144, 131915),
    (1, 69197, 18256, 233544, 18256, 17999, 225320, 233544, 87115),
    (1, 10032, 223264, 18256, 231488, 131658, 71952, 131401, 132172),
    (0, 83, 63, 63, 63, 47, 63, 31, 11),
    (1, 233544, 74008, 69896, 131915, 18256, 13887, 87115, 18184),
    (0, 95, 81, 81, 82, 82, 81, 81, 68),
    (1, 69968, 10032, 13887, 88914, 88914, 88657, 88657, 69896),
    (0, 0, 0, 1, 2, 0, 3, 5, 0),
    (0, 96, 136, 96, 96, 136, 136, 104, 88),
    (1, 12088, 133457, 133457, 13887, 227119, 32648, 24424, 217867),
    (1, 137055, 67840, 68097, 69896, 67840, 87629, 71952, 16128),
    (1, 70739, 13887, 17228, 132429, 32648, 131658, 223007, 74008),
    (0, 82, 68, 55, 70, 17, 39, 25, 9),
    (0, 111, 83, 82, 83, 55, 82, 63, 71),
    (1, 14144, 225320, 71952, 219152, 131915, 133714, 131658, 225320),
    (1, 219152, 133971, 219152, 89171, 72209, 7719, 13887, 132429),
    (1, 68683, 17228, 133714, 15686, 78120, 74008, 74265, 22296),
    (0, 17, 33, 68, 17, 63, 47, 47, 10),
    (0, 119, 69, 84, 47, 81, 83, 82, 69),
    (0, 1, 3, 4, 0, 4, 0, 6, 7),
    (0, 104, 96, 128, 120, 112, 120, 120, 96),
    (1, 26223, 76321, 76064, 10032, 11831, 227119, 28536, 76064),
    (1, 143223, 68611, 7976, 71952, 231231, 28536, 229432, 17927),
    (1, 131915, 227376, 134228, 132686, 227376, 229432, 9775, 132686),
    (1, 227376, 7976, 223264, 74008, 132429, 132172, 88914, 78120),
    (0, 25, 71, 70, 25, 69, 17, 67, 13),
    (0, 127, 84, 85, 55, 83, 68, 83, 70),
    (1, 74080, 134228, 11831, 68354, 13887, 68611, 133971, 34889),
    (0, 2, 1, 0, 1, 1, 1, 0, 3),
    (0, 112, 144, 136, 128, 104, 104, 136, 104),
    (1, 24424, 12088, 68868, 17485, 15429, 17742, 32648, 218381),
    (0, 9, 10, 71, 54, 71, 70, 54, 14),
    (1, 70482, 70410, 15172, 228918, 74008, 17999, 89171, 87372),
    (0, 63, 39, 91, 91, 90, 90, 84, 95),
    (1, 30335, 131658, 134485, 11574, 90970, 89171, 228918, 218638),
    (1, 132172, 229432, 15686, 132943, 229432, 233544, 131915, 160068),
    (0, 33, 17, 39, 9, 25, 71, 17, 17),
    (1, 219409, 16971, 225063, 17999, 132686, 132429, 89428, 16899),
    (0, 71, 47, 92, 71, 54, 84, 127, 54),
    (0, 23, 9, 9, 3, 2, 10, 1, 4),
    (0, 144, 104, 144, 136, 119, 112, 144, 83),
    (1, 13887, 70153, 70153, 72209, 88657, 18256, 34704, 87629),
    (1, 78192, 231231, 131658, 217353, 15943, 72209, 225320, 30006),
    (1, 132429, 17742, 225320, 133714, 233544, 132686, 132172, 228918),
    (1, 217353, 72209, 91227, 9775, 132943, 219152, 30335, 153927),
    (0, 42, 25, 17, 26, 61, 25, 30, 20),
    (0, 70, 55, 54, 67, 86, 127, 33, 111),
    (0, 47, 11, 10, 5, 3, 2, 2, 5),
    (1, 69454, 70667, 15943, 74265, 11574, 90970, 72209, 70153),
    (0, 88, 112, 88, 88, 135, 119, 103, 112),
    (1, 17999, 74265, 70410, 11831, 68868, 15172, 24167, 17156),
    (1, 86416, 5920, 11574, 91227, 89171, 70410, 74008, 70410),
    (0, 12, 41, 25, 31, 33, 34, 41, 12),
    (0, 87, 102, 67, 49, 39, 46, 111, 127),
    (1, 7976, 138854, 91484, 223007, 13373, 15686, 222750, 17413),
    (1, 132686, 132172, 131915, 133971, 133714, 221208, 133457, 137055),
    (1, 225834, 217610, 227376, 223264, 219152, 15943, 87372, 227376),
    (0, 19, 13, 31, 46, 12, 54, 49, 33),
    (0, 136, 95, 33, 99, 45, 91, 69, 38),
    (0, 3, 12, 12, 6, 5, 4, 11, 6),
    (0, 120, 120, 104, 126, 120, 128, 128, 85),
    (1, 72024, 15172, 16971, 70153, 74265, 87372, 30592, 72209),
    (1, 22368, 132429, 78120, 15943, 9261, 136027, 221208, 25894),
    (1, 132943, 218381, 231231, 136027, 133457, 231231, 26223, 141167),
    (1, 219923, 15429, 132429, 225320, 221208, 132943, 69125, 229432),
    (0, 18, 18, 11, 33, 68, 60, 70, 19),
    (0, 117, 118, 47, 59, 92, 92, 85, 135),
    (0, 4, 2, 13, 7, 6, 5, 3, 86),
    (0, 89, 128, 111, 81, 128, 144, 126, 113),
    (1, 80248, 78377, 17742, 74522, 87115, 30335, 30078, 89171),
    (1, 15943, 72466, 72209, 5920, 16971, 89428, 16971, 17670),
    (1, 3607, 71181, 74265, 93283, 28279, 28279, 69382, 72980),
    (0, 20, 19, 26, 61, 26, 62, 71, 49),
    (0, 66, 54, 66, 90, 70, 93, 86, 94),
    (1, 72281, 15943, 10032, 7976, 87629, 74265, 134742, 15217),
    (1, 133971, 219666, 228918, 231231, 133971, 225063, 133714, 145279),
    (1, 219666, 72723, 132686, 138083, 7719, 133457, 76321, 231488),
    (1, 15686, 7719, 22368, 80433, 76064, 76578, 17228, 70924),
    (0, 26, 70, 34, 13, 38, 26, 18, 15),
    (0, 67, 100, 69, 62, 99, 45, 59, 118),
    (0, 5, 30, 2, 10, 7, 6, 4, 89),
    (0, 81, 135, 112, 103, 144, 88, 112, 126),
    (1, 70225, 138340, 76321, 22368, 224806, 9518, 134228, 15961),
    (1, 133714, 219923, 136027, 229175, 229175, 226862, 219152, 147335),
    (1, 220180, 70924, 223007, 135770, 135770, 133971, 78377, 233544),
    (1, 9775, 9775, 14915, 14915, 15172, 11574, 14915, 76321),
    (0, 34, 31, 23, 45, 19, 33, 19, 81),
    (0, 68, 101, 100, 92, 46, 52, 61, 119),
    (0, 6, 4, 3, 11, 10, 19, 9, 23),
    (0, 114, 82, 120, 104, 88, 96, 102, 120),
    (1, 78706, 138597, 70924, 76321, 89942, 91227, 219923, 22039),
    (1, 27765, 76064, 70667, 9518, 15686, 13116, 80433, 89685),
    (0, 27, 49, 18, 34, 62, 36, 26, 25),
    (1, 221979, 11831, 5663, 90970, 76321, 91484, 15429, 218124),
    (0, 101, 87, 59, 66, 85, 85, 62, 117),
    (1, 145279, 132686, 217867, 226862, 228918, 228918, 145279, 136798),
    (1, 16714, 228918, 136284, 136284, 134742, 135770, 15686, 72723),
    (0, 50, 26, 35, 69, 23, 14, 92, 57),
    (0, 69, 62, 60, 84, 93, 66, 118, 102),
    (0, 7, 5, 5, 19, 9, 7, 14, 39),
    (0, 91, 85, 135, 112, 96, 135, 96, 128),
    (1, 72795, 23910, 71181, 30078, 9518, 13630, 89685, 26151),
    (1, 134999, 78120, 9775, 71181, 70924, 91741, 141167, 224806),
    (1, 229432, 132943, 138340, 134228, 225063, 226605, 227119, 169000),
    (1, 16971, 223007, 227119, 218381, 136284, 134228, 72466, 89942),
    (1, 65856, 22111, 74522, 12859, 13630, 9261, 15943, 26408),
    (0, 22, 14, 62, 39, 31, 15, 29, 26),
    (0, 59, 34, 108, 86, 34, 110, 110, 66),
    (0, 11, 28, 6, 27, 11, 9, 10, 55),
    (0, 90, 90, 126, 135, 110, 111, 91, 136),
    (1, 72538, 80176, 26223, 91484, 91484, 74522, 222493, 30263),
    (1, 32648, 75550, 16714, 13373, 7976, 76064, 72723, 80433),
    (1, 218124, 28022, 76578, 76578, 74522, 11060, 12859, 219923),
    (0, 28, 42, 30, 41, 43, 30, 21, 18),
    (0, 62, 61, 58, 87, 87, 42, 37, 67),
    (1, 142709, 218638, 140396, 226605, 138083, 145279, 220437, 131658),
    (1, 28536, 137055, 220951, 134742, 218124, 218638, 134485, 87886),
    (0, 21, 21, 38, 58, 58, 50, 42, 51),
    (0, 86, 38, 42, 95, 100, 59, 45, 58),
    (0, 10, 29, 19, 18, 18, 11, 12, 63),
    (0, 92, 91, 103, 127, 127, 118, 88, 144),
    (1, 73052, 11574, 17485, 80176, 93283, 6948, 26480, 32319),
    (1, 138597, 80433, 93540, 13630, 17742, 82232, 74522, 218895),
    (1, 221722, 220437, 222750, 134999, 226862, 218895, 136284, 158021),
    (1, 76136, 142966, 1037, 225063, 134485, 136541, 224549, 34632),
    (1, 14658, 1808, 72466, 9261, 26480, 16714, 91484, 69382),
    (0, 41, 20, 46, 22, 37, 58, 51, 28),
    (0, 102, 108, 99, 42, 101, 61, 94, 60),
    (0, 55, 6, 20, 20, 14, 18, 55, 22),
    (0, 99, 126, 83, 118, 126, 126, 101, 84),
    (1, 74851, 74522, 138083, 82232, 72723, 88914, 13373, 21782),
    (1, 14915, 3864, 14658, 16971, 102535, 76321, 23910, 100222),
    (1, 134742, 76578, 76835, 76064, 24424, 17485, 80176, 219666),
    (0, 49, 22, 22, 21, 102, 37, 28, 27),
    (0, 118, 65, 93, 38, 117, 94, 53, 61),
    (1, 223778, 224806, 136541, 220694, 136541, 222750, 226605, 155974),
    (1, 15172, 134999, 224806, 137055, 220951, 134485, 142966, 88657),
    (0, 57, 35, 86, 101, 35, 27, 36, 1),
    (0, 103, 66, 101, 102, 50, 53, 95, 62),
    (0, 15, 7, 28, 12, 20, 12, 39, 110),
    (0, 128, 103, 119, 85, 111, 117, 119, 148),
    (1, 82304, 32648, 15429, 5663, 12602, 1808, 82232, 8084),
    (1, 138854, 75036, 95596, 78120, 76578, 72723, 13630, 222236),
    (1, 227890, 220180, 138597, 220437, 134999, 224549, 222236, 142966),
    (1, 15429, 140396, 226862, 138597, 223007, 140910, 140910, 74265),
    (0, 39, 43, 43, 35, 41, 28, 43, 29),
    (0, 126, 127, 109, 65, 52, 31, 58, 50),
    (0, 45, 23, 36, 14, 27, 55, 13, 2),
    (0, 84, 86, 95, 117, 84, 86, 93, 91),
    (1, 70996, 22368, 12859, 88657, 96110, 78634, 28022, 16642),
    (1, 12859, 78634, 88143, 24167, 27765, 14658, 70667, 82489),
    (1, 220694, 15686, 82746, 14658, 78891, 80690, 21083, 221979),
    (1, 142966, 75293, 13116, 78377, 10546, 12859, 71438, 143223),
    (0, 58, 109, 45, 68, 53, 35, 27, 36),
    (0, 85, 111, 57, 108, 65, 69, 87, 103),
    (1, 13630, 220694, 134742, 138854, 224549, 221979, 136798, 74522),
    (0, 35, 27, 7, 4, 36, 101, 15, 41),
    (0, 135, 57, 65, 28, 91, 103, 65, 52),
    (0, 29, 46, 27, 15, 13, 21, 20, 87),
    (0, 98, 93, 102, 111, 118, 87, 109, 105),
    (1, 74594, 140653, 220694, 224806, 138597, 136798, 224292, 15465),
    (1, 222236, 76835, 13630, 15429, 11060, 82746, 78634, 222493),
    (1, 145022, 13630, 78634, 78634, 93540, 13373, 10803, 142709),
    (1, 30592, 221979, 140653, 222236, 224292, 222236, 137055, 80947),
    (0, 31, 44, 15, 57, 42, 57, 68, 65),
    (0, 43, 58, 41, 144, 66, 95, 135, 93),
    (0, 14, 15, 21, 23, 21, 13, 46, 90),
    (0, 106, 110, 110, 94, 95, 102, 117, 97),
    (1, 76650, 78891, 226605, 140396, 138854, 138597, 221979, 15713),
    (1, 134485, 13373, 78891, 12602, 11317, 76835, 23653, 138854),
    (1, 220437, 74779, 9518, 76835, 76835, 11317, 82746, 224292),
    (0, 37, 59, 49, 43, 22, 49, 7, 21),
    (0, 65, 117, 127, 60, 28, 65, 90, 53),
    (0, 51, 60, 87, 50, 51, 20, 34, 109),
    (0, 30, 88, 90, 119, 94, 108, 57, 46),
    (0, 122, 36, 29, 29, 15, 38, 38, 100),
    (1, 80762, 142709, 262144, 262144, 262144, 262144, 11317, 27950),
    (0, 60, 92, 118, 93, 103, 109, 100, 35),
    (0, 38, 50, 50, 51, 57, 23, 50, 82),
    (0, 46, 67, 61, 52, 59, 41, 66, 47),
    (0, 94, 37, 14, 30, 29, 22, 22, 99),
    (1, 73566, 79148, 262144, 262144, 262144, 262144, 8747, 28207),
    (0, 61, 94, 94, 110, 109, 99, 108, 43),
    (0, 44, 51, 51, 53, 60, 43, 35, 42),
    (0, 52, 53, 53, 109, 67, 51, 52, 92),
    (0, 54, 52, 44, 37, 44, 44, 44, 45),
    (0, 100, 119, 52, 44, 49, 67, 60, 101),
    (1, 75108, 262144, 262144, 262144, 262144, 262144, 262144, 27693),
    (0, 109, 45, 37, 36, 30, 29, 23, 59),
    (0, 36, 99, 117, 100, 108, 100, 99, 44),
    (0, 13, 262144, 262144, 262144, 262144, 262144, 262144, 30),
    (0, 93, 262144, 262144, 262144, 262144, 262144, 262144, 108),
    (0, 110, 262144, 262144, 262144, 262144, 262144, 262144, 31),
    (0, 53, 262144, 262144, 262144, 262144, 262144, 262144, 34),
    (0, 108, 262144, 262144, 262144, 262144, 262144, 262144, 37),
)
NONE = 2**18
OWN = BAND * HALF


def device_of(row, cols):
    return row // cols, lax.rem(row, cols)


def kernel(cols_ref, blocks_ref, out_ref, own, square, upper, flipped, newband, send_sem, recv_sem):
    size = blocks_ref.shape[-1]
    cols = lax.axis_size("col")
    count = cols * lax.axis_size("row")
    me = lax.axis_index("row") * cols + lax.axis_index("col")
    place = lax.rem(me, RING)
    start = me - place
    targets = (
        start + lax.rem(place + 1, RING),
        start + lax.rem(place + RING - 1, RING),
        lax.rem(me + RING, count),
        lax.rem(me + count - RING, count),
    )
    barrier = pltpu.get_barrier_semaphore()
    peers = [device_of(target, cols) for target in targets]
    for peer in peers:
        pl.semaphore_signal(barrier, inc=1, device_id=peer, device_id_type=MESH)

    bits = [lax.rem(place // 2**n, 2) == 1 for n in range(3)]

    def pick(values):
        for bit in bits:
            values = [jnp.where(bit, high, low) for low, high in zip(values[::2], values[1::2])]
        return values[0]

    missing = jnp.int32(0)
    for s in range(WINDOW - 1):
        offset = lax.rem(cols_ref[0, s] - me + BAND + count, count)
        missing += jnp.where(offset == s, 1, 0)

    for o in range(WINDOW):
        first = blocks_ref[0, min(o, WINDOW - 2)]
        second = blocks_ref[0, max(o - 1, 0)]
        block = jnp.where(o < missing, first, jnp.where(o == missing, jnp.zeros_like(first), second))
        own[:, o * size : (o + 1) * size] = block
        turned = block.T
        if o >= BAND:
            upper[OWN + o - BAND] = block
            flipped[OWN + o - BAND] = turned
        else:
            slot = o * HALF + BAND - o
            upper[slot] = turned
            flipped[slot] = block

    pl.semaphore_wait(barrier, len(targets))

    def copy(n, here, there, peer):
        return pltpu.make_async_remote_copy(
            src_ref=upper.at[here],
            dst_ref=upper.at[there],
            send_sem=send_sem.at[n],
            recv_sem=recv_sem.at[there],
            device_id=peer,
            device_id_type=MESH,
        )

    def send(n, code):
        direction = code >> 16
        ahead, far = (direction & 1) == 0, direction >= 2
        peer = tuple(
            jnp.where(far, jnp.where(ahead, c, d), jnp.where(ahead, a, b)) for a, b, c, d in zip(*peers)
        )
        copy(n, code & 255, (code >> 8) & 255, peer).start()

    def receive(here):
        copy(0, here, here, peers[0]).wait_recv()
        flipped[here] = upper[here].T

    def where_any(codes, code, action):
        if NONE in codes:
            pl.when(code != NONE)(action)
        else:
            action()

    sent = []
    for sends, *codes in EVENTS:
        code = pick([jnp.int32(c) for c in codes])
        if sends:
            where_any(codes, code, functools.partial(send, len(sent), code))
            sent.append((codes, code))
        else:
            where_any(codes, code, functools.partial(receive, code))

    def block_at(k, j):
        if abs(k - j) > BAND:
            return jnp.zeros((size, size), upper.dtype)
        return upper[k * HALF + j - k] if k <= j else flipped[j * HALF + k - j]

    def product(factor, first, width):
        low, high = max(0, first - BAND), min(WINDOW, first + width + BAND)
        columns = [
            jnp.concatenate([block_at(k, j) for k in range(low, high)], axis=0) for j in range(first, first + width)
        ]
        return jnp.dot(
            factor[:, low * size : high * size],
            jnp.concatenate(columns, axis=1),
            preferred_element_type=jnp.float32,
        )

    for first in range(0, WINDOW, 2):
        width = min(2, WINDOW - first)
        total = product(own, first, width)
        for w in range(width):
            piece = total[:, w * size : (w + 1) * size]
            piece = jnp.where(missing == first + w, 0.0, piece).astype(square.dtype)
            square[:, (first + w) * size : (first + w + 1) * size] = piece
    for first in range(0, WINDOW, 2):
        width = min(2, WINDOW - first)
        total = product(square, first, width)
        for w in range(width):
            part = slice((first + w) * size, (first + w + 1) * size)
            value = 3.0 * square[:, part].astype(jnp.float32) - 2.0 * total[:, w * size : (w + 1) * size]
            newband[first + w] = value.astype(newband.dtype)
    for s in range(WINDOW - 1):
        out_ref[0, s] = jnp.where(s < missing, newband[s], newband[s + 1])

    for n, (codes, code) in enumerate(sent):
        where_any(codes, code, lambda n=n: copy(n, OWN, OWN, peers[0]).wait_send())


def per_device(block_cols, blocks):
    size = blocks.shape[-1]
    kind = blocks.dtype
    sends = sum(event[0] for event in EVENTS)
    return pl.pallas_call(
        kernel,
        out_shape=jax.ShapeDtypeStruct(blocks.shape, kind),
        in_specs=[pl.BlockSpec(memory_space=pltpu.SMEM), pl.BlockSpec(memory_space=pltpu.VMEM)],
        out_specs=pl.BlockSpec(memory_space=pltpu.VMEM),
        scratch_shapes=[
            pltpu.VMEM((size, WINDOW * size), kind),
            pltpu.VMEM((size, WINDOW * size), kind),
            pltpu.VMEM((WINDOW * HALF, size, size), kind),
            pltpu.VMEM((WINDOW * HALF, size, size), kind),
            pltpu.VMEM((WINDOW, size, size), kind),
            pltpu.SemaphoreType.DMA((sends,)),
            pltpu.SemaphoreType.DMA((WINDOW * HALF,)),
        ],
        compiler_params=pltpu.CompilerParams(collective_id=0, has_side_effects=True, vmem_limit_bytes=40 * 2**20),
        cost_estimate=pl.CostEstimate(flops=4 * 217 * size**3, bytes_accessed=2 * 2**20, transcendentals=0),
        name="purify",
    )(block_cols, blocks)


def solution(mesh):
    placed = (P(("row", "col"), None), P(("row", "col"), None, None, None))
    return jax.shard_map(
        per_device,
        mesh=mesh,
        in_specs=placed,
        out_specs=P(("row", "col"), None, None, None),
        check_vma=False,
    )
```

```python
import functools

import jax
import jax.numpy as jnp
from jax import lax
from jax.experimental import pallas as pl
from jax.experimental.pallas import tpu as pltpu
from jax.sharding import PartitionSpec as P

BAND = 8
WINDOW = 2 * BAND + 1
HALF = BAND + 1
RING = 8
MESH = pl.DeviceIdType.MESH

EVENTS = (
    (1, 16200, 231488, 229432, 231488, 225320, 223264, 221208, 223264),
    (1, 67912, 14144, 14144, 14144, 7976, 86344, 12088, 34632),
    (1, 131144, 86344, 86344, 86344, 86344, 16200, 86344, 86344),
    (1, 219152, 132429, 131915, 131401, 131144, 131915, 131144, 132943),
    (1, 68169, 16200, 16200, 16200, 14144, 14144, 14144, 32576),
    (1, 14144, 86601, 86601, 86601, 86601, 86601, 86601, 86601),
    (1, 233544, 233544, 231488, 227376, 227376, 229432, 223264, 169248),
    (1, 131401, 131144, 132172, 132429, 131401, 131144, 131401, 225320),
    (1, 68426, 86858, 86858, 86858, 16200, 86858, 16200, 26408),
    (1, 17742, 18256, 18256, 17742, 69896, 17228, 69896, 69896),
    (1, 233801, 131401, 12088, 229432, 10032, 225320, 225320, 71952),
    (1, 131658, 17999, 233544, 131144, 229432, 131401, 86858, 227376),
    (1, 17999, 69896, 132429, 87115, 86858, 17999, 131658, 28464),
    (1, 69968, 219152, 69896, 17999, 131658, 69896, 22792, 132429),
    (1, 131915, 71952, 17742, 18256, 12088, 18256, 87115, 74008),
    (1, 221208, 131658, 74008, 233544, 87115, 71952, 229432, 30520),
    (1, 68683, 221208, 131401, 131658, 231488, 131658, 131915, 229432),
    (1, 18256, 10032, 219152, 10032, 131915, 10032, 10032, 132686),
    (1, 223264, 87115, 17999, 69896, 17485, 233544, 71952, 86858),
    (1, 10032, 223264, 76064, 12088, 71952, 87115, 231488, 18184),
    (1, 12088, 12088, 221208, 131915, 233544, 132172, 17228, 169744),
    (1, 17228, 87372, 10032, 219152, 17999, 74008, 132172, 231488),
    (1, 132172, 131915, 131144, 71952, 74008, 132429, 17742, 87115),
    (0, 81, 63, 55, 55, 55, 31, 63, 9),
    (1, 70225, 225320, 223264, 74008, 18256, 227376, 233544, 168504),
    (0, 135, 81, 81, 81, 81, 81, 81, 47),
    (1, 32391, 80176, 131658, 132172, 132172, 132686, 132429, 233544),
    (1, 68940, 17485, 225320, 221208, 219152, 223007, 17999, 168256),
    (1, 17485, 227376, 88657, 76064, 132429, 88657, 74008, 28207),
    (0, 0, 5, 3, 1, 0, 3, 0, 7),
    (0, 88, 136, 128, 136, 112, 104, 96, 104),
    (1, 72024, 13887, 133457, 132686, 221208, 76064, 132686, 70153),
    (1, 132429, 88657, 11831, 223264, 88657, 17742, 13887, 17927),
    (1, 235343, 17742, 68611, 88657, 11831, 24424, 88657, 131144),
    (0, 82, 55, 63, 63, 63, 55, 55, 10),
    (1, 70482, 132172, 132686, 11831, 132686, 231488, 76064, 70410),
    (0, 127, 82, 82, 82, 82, 82, 82, 55),
    (1, 30335, 229432, 227376, 17485, 88914, 132943, 227376, 30263),
    (0, 1, 0, 4, 5, 1, 0, 1, 11),
    (1, 3864, 11831, 13887, 132943, 13887, 11831, 132943, 70667),
    (0, 83, 69, 71, 17, 69, 17, 17, 63),
    (0, 103, 83, 83, 71, 83, 63, 67, 112),
    (1, 139111, 88914, 88914, 225320, 133971, 88914, 88914, 32319),
    (1, 70739, 3864, 17228, 13887, 89171, 78120, 11831, 22296),
    (0, 144, 144, 136, 120, 120, 128, 104, 149),
    (1, 86416, 133971, 68868, 88914, 15429, 231231, 87372, 76064),
    (1, 5920, 89171, 15943, 87372, 132943, 30592, 72209, 131658),
    (0, 17, 17, 70, 47, 17, 39, 25, 17),
    (1, 225320, 231231, 89171, 5920, 223264, 13887, 14915, 72209),
    (0, 111, 70, 84, 83, 70, 83, 70, 89),
    (1, 141167, 132686, 229175, 15943, 72209, 72209, 133457, 15961),
    (1, 219409, 5920, 17485, 72209, 15686, 133457, 87629, 6037),
    (1, 7976, 72209, 133971, 229175, 87372, 87372, 15686, 78120),
    (0, 2, 1, 5, 0, 2, 1, 2, 5),
    (0, 145, 88, 144, 128, 128, 112, 112, 120),
    (1, 86673, 7976, 71952, 133457, 17228, 221208, 22368, 131915),
    (0, 25, 33, 54, 69, 25, 47, 33, 18),
    (1, 227376, 132943, 89428, 78120, 231231, 7719, 87886, 219666),
    (0, 119, 126, 90, 84, 71, 84, 71, 54),
    (1, 221465, 229175, 5920, 7976, 133457, 87629, 133714, 228918),
    (1, 28279, 30078, 231231, 32648, 74265, 26480, 223521, 72466),
    (0, 3, 2, 1, 2, 3, 2, 3, 6),
    (0, 71, 41, 17, 25, 39, 25, 39, 12),
    (0, 90, 71, 39, 70, 90, 68, 83, 39),
    (1, 72538, 145022, 134228, 89171, 15943, 133714, 15943, 30006),
    (0, 96, 96, 88, 144, 136, 103, 128, 128),
    (1, 74080, 76321, 11574, 231231, 87629, 9775, 74265, 87372),
    (1, 132686, 15429, 90970, 133714, 17742, 87886, 24424, 17413),
    (1, 229432, 78377, 69125, 9775, 90970, 24167, 76321, 218124),
    (1, 15943, 15686, 7976, 89428, 225063, 229175, 26480, 225063),
    (0, 84, 39, 25, 33, 47, 70, 84, 25),
    (1, 70996, 69125, 228918, 227119, 133714, 15172, 133971, 26151),
    (0, 110, 90, 47, 39, 84, 90, 95, 67),
    (1, 25966, 90970, 135770, 133971, 76064, 89171, 7719, 132172),
    (0, 31, 11, 9, 3, 11, 4, 4, 136),
    (0, 104, 104, 96, 88, 144, 144, 136, 151),
    (1, 76136, 225063, 15686, 15429, 5920, 133971, 89171, 87629),
    (1, 135770, 15943, 72209, 74265, 227119, 15686, 137055, 87886),
    (0, 70, 12, 33, 46, 33, 71, 18, 19),
    (0, 85, 47, 46, 90, 46, 91, 46, 69),
    (1, 71253, 70924, 74265, 15686, 7719, 89428, 219152, 17670),
    (1, 15686, 218124, 7719, 76321, 89428, 225063, 226862, 162115),
    (0, 39, 3, 0, 4, 4, 5, 5, 20),
    (0, 57, 91, 41, 54, 54, 26, 19, 70),
    (0, 89, 112, 104, 91, 88, 46, 119, 144),
    (0, 118, 118, 117, 96, 91, 135, 144, 146),
    (1, 142966, 7719, 225063, 134228, 135770, 134228, 22111, 219923),
    (1, 229689, 91227, 76321, 225063, 226862, 15943, 89428, 70924),
    (1, 72281, 133457, 9775, 90970, 9518, 74265, 72466, 1943),
    (1, 134228, 227119, 78377, 7719, 76321, 9518, 28279, 220180),
    (0, 91, 13, 68, 62, 26, 33, 20, 27),
    (0, 126, 67, 91, 92, 62, 54, 54, 46),
    (1, 145022, 9775, 9518, 226862, 228918, 227119, 229175, 74265),
    (1, 72795, 71181, 227119, 9518, 11574, 90970, 134228, 158021),
    (1, 16971, 28022, 136027, 135770, 91227, 135770, 220180, 221979),
    (0, 4, 54, 2, 6, 5, 6, 6, 90),
    (0, 97, 120, 112, 104, 96, 120, 105, 145),
    (1, 74337, 74008, 91227, 91227, 136027, 228918, 72723, 27950),
    (1, 140910, 218381, 27765, 11574, 13630, 91227, 11574, 72723),
    (0, 62, 68, 26, 26, 41, 41, 26, 13),
    (1, 230974, 136027, 226862, 91484, 74522, 136027, 225063, 12178),
    (0, 92, 92, 69, 45, 68, 60, 69, 58),
    (1, 73052, 136284, 16714, 228918, 78120, 13116, 143223, 226862),
    (1, 24167, 16714, 74522, 136027, 16714, 74522, 72980, 155974),
    (0, 5, 4, 6, 7, 6, 7, 7, 0),
    (0, 26, 15, 15, 34, 23, 61, 27, 61),
    (0, 117, 99, 85, 67, 49, 85, 30, 81),
    (1, 27765, 76064, 134485, 13630, 220951, 13373, 17485, 72980),
    (1, 221722, 138083, 82232, 74522, 80176, 80176, 221979, 14225),
    (0, 151, 128, 120, 112, 119, 136, 120, 126),
    (1, 134485, 67840, 16971, 226605, 16971, 134485, 222750, 218381),
    (0, 42, 23, 23, 68, 31, 62, 41, 62),
    (0, 87, 25, 49, 99, 85, 86, 103, 82),
    (1, 26223, 16971, 218895, 9261, 134485, 13630, 30592, 80176),
    (1, 225834, 142966, 3864, 76578, 223007, 16971, 74522, 16128),
    (1, 5663, 218895, 78120, 138083, 9775, 68611, 139111, 164410),
    (1, 65856, 68097, 220951, 16714, 87886, 134742, 78120, 82232),
    (0, 46, 6, 11, 9, 7, 9, 9, 2),
    (0, 112, 135, 127, 127, 104, 96, 118, 84),
    (0, 23, 31, 31, 23, 86, 67, 38, 33),
    (0, 50, 93, 92, 85, 127, 87, 49, 87),
    (1, 136027, 17228, 136284, 93283, 134742, 76321, 32648, 16642),
    (1, 227890, 220951, 15172, 134485, 70667, 17485, 224806, 158269),
    (1, 88215, 136541, 80176, 220951, 15172, 78377, 80176, 74779),
    (0, 54, 7, 12, 10, 9, 10, 10, 3),
    (0, 68, 14, 60, 31, 38, 34, 85, 21),
    (0, 99, 110, 93, 86, 87, 69, 92, 95),
    (1, 7719, 68354, 136541, 80176, 224806, 34704, 34704, 220437),
    (0, 120, 127, 135, 135, 135, 126, 94, 99),
    (1, 74851, 1808, 15429, 16971, 134999, 134999, 136798, 16899),
    (0, 14, 26, 34, 41, 60, 23, 59, 41),
    (1, 142709, 14915, 68097, 17228, 78377, 220951, 24681, 88657),
    (1, 28022, 70667, 223007, 87629, 28279, 32391, 88143, 156222),
    (0, 102, 62, 61, 61, 92, 42, 86, 103),
    (1, 78192, 140910, 70153, 134742, 136284, 89685, 134485, 88914),
    (0, 6, 20, 18, 11, 10, 11, 11, 4),
    (0, 128, 111, 126, 119, 111, 127, 99, 111),
    (0, 21, 34, 42, 30, 61, 30, 61, 22),
    (1, 231488, 223007, 5663, 223007, 80433, 222750, 74779, 17156),
    (0, 69, 101, 62, 93, 93, 92, 87, 30),
    (1, 30078, 91484, 13116, 14915, 5663, 136284, 15429, 134999),
    (1, 80248, 11574, 80433, 68097, 136541, 76578, 134742, 220694),
    (0, 18, 27, 19, 12, 18, 12, 21, 26),
    (0, 100, 42, 30, 38, 30, 37, 23, 86),
    (0, 109, 61, 99, 42, 34, 93, 62, 91),
    (1, 134999, 218638, 138083, 136541, 30335, 11574, 78377, 222750),
    (1, 220951, 138597, 222750, 222750, 89685, 224549, 28022, 76321),
    (0, 129, 84, 111, 111, 118, 111, 88, 121),
    (1, 82304, 15172, 13373, 15172, 222750, 78634, 220437, 14969),
    (1, 13630, 74265, 76578, 69125, 13116, 14915, 21340, 137055),
    (0, 7, 50, 38, 37, 37, 27, 34, 28),
    (0, 22, 108, 100, 100, 99, 45, 37, 110),
    (1, 218638, 74522, 138340, 89685, 91484, 136541, 80433, 93283),
    (1, 138083, 5663, 224806, 5663, 224549, 221979, 134999, 222236),
    (1, 75108, 140396, 13630, 224806, 138083, 226605, 224549, 78377),
    (0, 12, 9, 13, 18, 19, 18, 12, 92),
    (0, 134, 119, 119, 118, 126, 119, 127, 105),
    (1, 9518, 72980, 78634, 138340, 13373, 30078, 12859, 15465),
    (0, 33, 66, 101, 35, 45, 28, 28, 34),
    (1, 11574, 13630, 138597, 13373, 76578, 91484, 89685, 139111),
    (0, 47, 100, 109, 108, 100, 53, 51, 45),
    (1, 82561, 138340, 140653, 78377, 226605, 222236, 222236, 27693),
    (1, 220437, 76578, 7462, 224549, 138340, 15429, 93283, 226605),
    (0, 38, 19, 20, 19, 13, 19, 29, 29),
    (0, 41, 35, 35, 49, 35, 29, 47, 68),
    (0, 55, 85, 65, 65, 53, 65, 52, 97),
    (1, 138854, 13373, 76835, 140396, 11317, 222493, 13373, 74522),
    (0, 98, 94, 118, 126, 95, 95, 111, 118),
    (0, 9, 65, 43, 57, 36, 35, 53, 36),
    (1, 83846, 74779, 78891, 7462, 76835, 11317, 222493, 15713),
    (0, 63, 102, 66, 66, 57, 66, 57, 119),
    (0, 13, 46, 21, 27, 14, 13, 31, 85),
    (0, 114, 87, 87, 117, 103, 102, 102, 130),
    (0, 10, 22, 67, 15, 12, 38, 65, 1),
    (0, 65, 49, 108, 87, 65, 49, 66, 127),
    (1, 15172, 78634, 140396, 78634, 224292, 76835, 76578, 134742),
    (1, 220694, 80690, 262144, 76835, 262144, 262144, 13630, 222493),
    (1, 138340, 76835, 262144, 262144, 262144, 262144, 10803, 76578),
    (1, 74594, 262144, 262144, 262144, 262144, 262144, 11060, 12674),
    (1, 15429, 262144, 262144, 262144, 262144, 262144, 11317, 224292),
    (1, 78706, 262144, 262144, 262144, 262144, 262144, 262144, 140910),
    (0, 11, 21, 7, 13, 15, 14, 22, 88),
    (0, 19, 30, 27, 20, 42, 57, 36, 93),
    (0, 66, 57, 57, 59, 66, 59, 68, 106),
    (1, 140653, 262144, 262144, 262144, 262144, 262144, 262144, 13418),
    (0, 122, 95, 95, 95, 110, 109, 110, 135),
    (0, 20, 10, 58, 50, 50, 88, 90, 49),
    (0, 67, 109, 86, 60, 67, 110, 135, 96),
    (0, 45, 38, 28, 14, 20, 15, 13, 94),
    (0, 136, 103, 103, 103, 102, 99, 93, 98),
    (1, 80762, 262144, 262144, 262144, 262144, 262144, 262144, 13666),
    (0, 58, 18, 10, 22, 58, 22, 91, 57),
    (0, 101, 117, 45, 58, 94, 36, 126, 60),
    (0, 15, 29, 14, 21, 21, 20, 14, 15),
    (0, 34, 53, 29, 51, 43, 50, 42, 65),
    (0, 60, 58, 59, 94, 59, 117, 45, 102),
    (0, 95, 86, 102, 102, 109, 118, 109, 109),
    (0, 35, 37, 22, 52, 22, 51, 58, 37),
    (0, 108, 43, 94, 101, 51, 58, 108, 83),
    (0, 27, 36, 37, 28, 27, 21, 15, 23),
    (0, 86, 45, 110, 110, 117, 100, 100, 100),
    (0, 29, 51, 50, 43, 52, 52, 50, 50),
    (0, 61, 28, 53, 53, 101, 94, 117, 66),
    (0, 30, 44, 36, 29, 28, 44, 35, 31),
    (0, 43, 59, 51, 36, 29, 101, 60, 52),
    (0, 49, 52, 52, 44, 44, 108, 101, 71),
    (0, 93, 60, 44, 109, 108, 43, 43, 117),
    (0, 36, 262144, 262144, 262144, 262144, 262144, 44, 35),
    (0, 52, 262144, 262144, 262144, 262144, 262144, 262144, 53),
    (0, 28, 262144, 262144, 262144, 262144, 262144, 262144, 14),
    (0, 94, 262144, 262144, 262144, 262144, 262144, 262144, 101),
    (0, 51, 262144, 262144, 262144, 262144, 262144, 262144, 42),
    (0, 53, 262144, 262144, 262144, 262144, 262144, 262144, 51),
    (0, 37, 262144, 262144, 262144, 262144, 262144, 262144, 38),
    (0, 59, 262144, 262144, 262144, 262144, 262144, 262144, 43),
    (0, 44, 262144, 262144, 262144, 262144, 262144, 262144, 59),
    (0, 262144, 262144, 262144, 262144, 262144, 262144, 262144, 108),
    (0, 262144, 262144, 262144, 262144, 262144, 262144, 262144, 44),
)
NONE = 2**18
OWN = BAND * HALF


def device_of(row, cols):
    return row // cols, lax.rem(row, cols)


def kernel(cols_hbm, blocks_hbm, out_ref, cols_ref, blocks_ref, own, square, upper, flipped, newband, in_sem, send_sem, recv_sem):
    size = blocks_ref.shape[-1]
    loads = [
        pltpu.make_async_copy(cols_hbm, cols_ref, in_sem.at[0]),
        pltpu.make_async_copy(blocks_hbm, blocks_ref, in_sem.at[1]),
    ]
    for load in loads:
        load.start()
    cols = lax.axis_size("col")
    count = cols * lax.axis_size("row")
    me = lax.axis_index("row") * cols + lax.axis_index("col")
    place = lax.rem(me, RING)
    start = me - place
    targets = (
        start + lax.rem(place + 1, RING),
        start + lax.rem(place + RING - 1, RING),
        lax.rem(me + RING, count),
        lax.rem(me + count - RING, count),
    )
    barrier = pltpu.get_barrier_semaphore()
    peers = [device_of(target, cols) for target in targets]
    for peer in peers:
        pl.semaphore_signal(barrier, inc=1, device_id=peer, device_id_type=MESH)

    bits = [lax.rem(place // 2**n, 2) == 1 for n in range(3)]

    def pick(values):
        for bit in bits:
            values = [jnp.where(bit, high, low) for low, high in zip(values[::2], values[1::2])]
        return values[0]

    for load in loads:
        load.wait()
    missing = jnp.int32(0)
    for s in range(WINDOW - 1):
        offset = lax.rem(cols_ref[0, s] - me + BAND + count, count)
        missing += jnp.where(offset == s, 1, 0)

    for o in range(WINDOW):
        first = blocks_ref[0, min(o, WINDOW - 2)]
        second = blocks_ref[0, max(o - 1, 0)]
        block = jnp.where(o < missing, first, jnp.where(o == missing, jnp.zeros_like(first), second))
        own[:, o * size : (o + 1) * size] = block
        turned = block.T
        if o >= BAND:
            upper[OWN + o - BAND] = block
            flipped[OWN + o - BAND] = turned
        else:
            slot = o * HALF + BAND - o
            upper[slot] = turned
            flipped[slot] = block

    pl.semaphore_wait(barrier, len(targets))

    def copy(n, here, there, peer):
        return pltpu.make_async_remote_copy(
            src_ref=upper.at[here],
            dst_ref=upper.at[there],
            send_sem=send_sem.at[n],
            recv_sem=recv_sem.at[there],
            device_id=peer,
            device_id_type=MESH,
        )

    def send(n, code):
        direction = code >> 16
        ahead, far = (direction & 1) == 0, direction >= 2
        peer = tuple(
            jnp.where(far, jnp.where(ahead, c, d), jnp.where(ahead, a, b)) for a, b, c, d in zip(*peers)
        )
        copy(n, code & 255, (code >> 8) & 255, peer).start()

    def receive(here):
        copy(0, here, here, peers[0]).wait_recv()
        flipped[here] = upper[here].T

    def where_any(codes, code, action):
        if NONE in codes:
            pl.when(code != NONE)(action)
        else:
            action()

    sent = []
    for sends, *codes in EVENTS:
        code = pick([jnp.int32(c) for c in codes])
        if sends:
            where_any(codes, code, functools.partial(send, len(sent), code))
            sent.append((codes, code))
        else:
            where_any(codes, code, functools.partial(receive, code))

    def block_at(k, j):
        if abs(k - j) > BAND:
            return jnp.zeros((size, size), upper.dtype)
        return upper[k * HALF + j - k] if k <= j else flipped[j * HALF + k - j]

    def product(factor, first, width):
        low, high = max(0, first - BAND), min(WINDOW, first + width + BAND)
        columns = [
            jnp.concatenate([block_at(k, j) for k in range(low, high)], axis=0) for j in range(first, first + width)
        ]
        return jnp.dot(
            factor[:, low * size : high * size],
            jnp.concatenate(columns, axis=1),
            preferred_element_type=jnp.float32,
        )

    for first in range(0, WINDOW, 2):
        width = min(2, WINDOW - first)
        total = product(own, first, width)
        for w in range(width):
            piece = total[:, w * size : (w + 1) * size]
            piece = jnp.where(missing == first + w, 0.0, piece).astype(square.dtype)
            square[:, (first + w) * size : (first + w + 1) * size] = piece
    for first in range(0, WINDOW, 2):
        width = min(2, WINDOW - first)
        total = product(square, first, width)
        for w in range(width):
            part = slice((first + w) * size, (first + w + 1) * size)
            value = 3.0 * square[:, part].astype(jnp.float32) - 2.0 * total[:, w * size : (w + 1) * size]
            newband[first + w] = value.astype(newband.dtype)
    for s in range(WINDOW - 1):
        out_ref[0, s] = jnp.where(s < missing, newband[s], newband[s + 1])

    for n, (codes, code) in enumerate(sent):
        where_any(codes, code, lambda n=n: copy(n, OWN, OWN, peers[0]).wait_send())


def per_device(block_cols, blocks):
    size = blocks.shape[-1]
    kind = blocks.dtype
    sends = sum(event[0] for event in EVENTS)
    return pl.pallas_call(
        kernel,
        out_shape=jax.ShapeDtypeStruct(blocks.shape, kind),
        in_specs=[pl.BlockSpec(memory_space=pltpu.HBM)] * 2,
        out_specs=pl.BlockSpec(memory_space=pltpu.VMEM),
        scratch_shapes=[
            pltpu.SMEM(block_cols.shape, block_cols.dtype),
            pltpu.VMEM(blocks.shape, kind),
            pltpu.VMEM((size, WINDOW * size), kind),
            pltpu.VMEM((size, WINDOW * size), kind),
            pltpu.VMEM((WINDOW * HALF, size, size), kind),
            pltpu.VMEM((WINDOW * HALF, size, size), kind),
            pltpu.VMEM((WINDOW, size, size), kind),
            pltpu.SemaphoreType.DMA((2,)),
            pltpu.SemaphoreType.DMA((sends,)),
            pltpu.SemaphoreType.DMA((WINDOW * HALF,)),
        ],
        compiler_params=pltpu.CompilerParams(collective_id=0, has_side_effects=True, vmem_limit_bytes=40 * 2**20),
        cost_estimate=pl.CostEstimate(flops=4 * 217 * size**3, bytes_accessed=2 * 2**20, transcendentals=0),
        name="purify",
    )(*(pltpu.with_memory_space_constraint(x, pltpu.HBM) for x in (block_cols, blocks)))


def solution(mesh):
    placed = (P(("row", "col"), None), P(("row", "col"), None, None, None))
    return jax.shard_map(
        per_device,
        mesh=mesh,
        in_specs=placed,
        out_specs=P(("row", "col"), None, None, None),
        check_vma=False,
    )
```

```python
import functools

import jax
import jax.numpy as jnp
from jax import lax
from jax.experimental import pallas as pl
from jax.experimental.pallas import tpu as pltpu
from jax.sharding import PartitionSpec as P

BAND = 8
WINDOW = 2 * BAND + 1
HALF = BAND + 1
RING = 8
MESH = pl.DeviceIdType.MESH

NONE = 2**18
EVENTS = (
    (
        (1, 16200, 14144, 14144, 86344, 86344, 86344, 86344, 168504),
        (1, 67912, 86344, 86344, 16200, 16200, 16200, 16200, 32576),
        (1, 131144, 132429, 131915, 131658, 131144, 131144, 131144, 86344),
        (1, 69968, 16200, 16200, 14144, 12088, 14144, 12088, 34632),
        (1, 12088, 86601, 86601, 86601, 86601, 86601, 86601, 86601),
        (1, 131401, 131401, 131144, 131144, 131401, 131401, 131401, 169000),
        (1, 68169, 86858, 86858, 86858, 10032, 86858, 14144, 18184),
        (1, 14144, 18256, 17999, 18256, 86858, 18256, 71952, 69896),
        (1, 131658, 131658, 131401, 10032, 131658, 10032, 10032, 26408),
        (1, 68683, 69896, 87372, 131401, 87115, 131658, 131658, 168752),
        (1, 17999, 12088, 18256, 87115, 17999, 69896, 69896, 86858),
        (1, 68940, 87115, 12088, 12088, 18256, 12088, 86858, 28464),
        (1, 18256, 17999, 69896, 87372, 69896, 71952, 17999, 87115),
        (2,),
        (1, 233801, 231488, 229432, 223264, 231488, 225320, 223264, 219152),
        (1, 131915, 132172, 131658, 131915, 131915, 131915, 131915, 168256),
        (1, 234058, 233544, 17742, 17742, 132172, 231488, 221208, 87372),
        (1, 132172, 131144, 231488, 227376, 71952, 132172, 87115, 221208),
        (1, 7976, 10032, 132172, 132172, 225320, 17485, 132172, 131144),
        (1, 219152, 71952, 10032, 17999, 132429, 74008, 87372, 87629),
        (1, 132429, 219152, 132429, 229432, 7976, 132429, 227376, 87886),
        (1, 68426, 74008, 71952, 132429, 74008, 17742, 132429, 223264),
        (1, 10032, NONE, NONE, NONE, NONE, NONE, 7976, 169744),
        (1, NONE, NONE, NONE, NONE, NONE, NONE, 87629, 71952),
        (0, 81, 63, 55, 55, 63, 63, 63, 9),
        (0, 127, 81, 81, 81, 81, 81, 81, 63),
        (1, 70225, 13887, 88657, 88657, 13887, 13887, 13887, 32319),
        (1, 30335, 88657, 11831, 11831, 88657, 88657, 88657, 225320),
        (1, 233544, 221208, 233544, 231488, 227376, 231231, 229432, 74008),
        (1, 17228, 16971, 133457, 132686, 14144, 223264, 87886, 169496),
        (1, 69197, 76064, 74008, 69896, 132686, 87115, 132686, 30520),
        (1, 132686, NONE, NONE, NONE, NONE, 132686, 22792, NONE),
        (1, NONE, NONE, NONE, NONE, NONE, 17999, NONE, NONE),
        (0, 82, 47, 63, 63, 55, 47, 55, 17),
        (0, 135, 82, 82, 82, 82, 82, 82, 47),
        (1, 70482, 88914, 88914, 88914, 229175, 9775, 11831, 28207),
        (1, 32391, 9775, 13887, 13887, 11831, 88914, 88914, 70153),
        (1, 221208, 223264, 87629, 233544, 88914, 227376, 231231, 169248),
        (1, NONE, 131915, 219152, NONE, 229432, 132943, 132943, NONE),
        (1, NONE, NONE, NONE, NONE, 132943, NONE, NONE, NONE),
        (0, 71, 55, 71, 70, 71, 25, 17, 10),
        (0, 83, 83, 83, 83, 83, 39, 71, 55),
        (1, 70739, 133971, 89171, 89171, 15943, 74265, 15943, 30263),
        (1, 17485, 11831, 15943, 15686, 89171, 7719, 74008, 72209),
        (1, NONE, NONE, NONE, 17485, 17228, 87372, NONE, NONE),
        (1, NONE, NONE, NONE, 71952, NONE, NONE, NONE, NONE),
        (0, 17, 70, 47, 71, 17, 17, 39, 12),
        (0, 103, 85, 84, 84, 39, 70, 83, 39),
        (1, 223264, 134485, 227119, 89428, 133457, 229432, 225063, 26151),
        (1, 133457, 225320, 9775, 15943, 17485, 133457, 133457, 227376),
        (1, NONE, 17485, 89428, 221208, 76064, 15686, 72209, 131658),
        (1, NONE, 78120, 221208, 132943, NONE, 87629, NONE, NONE),
        (1, NONE, NONE, 17485, 74008, NONE, NONE, NONE, NONE),
        (1, NONE, NONE, 133714, 7976, NONE, NONE, NONE, NONE),
        (0, 84, 17, 70, 17, 25, 71, 47, 13),
        (0, 111, 71, 85, 47, 47, 83, 84, 70),
        (1, 17742, 17742, 87115, 9775, 17742, 15943, 9775, 76064),
        (1, 219409, 72209, 5920, 76064, 72209, 72209, 76064, 131915),
        (1, 134228, 227376, 223264, 133457, 233544, 233544, 133714, NONE),
        (1, NONE, 132686, 134228, NONE, 133714, 133714, NONE, NONE),
        (0, 0, 5, 3, 2, 0, 0, 0, 88),
        (0, 145, 136, 128, 104, 136, 112, 104, 146),
        (1, 86673, NONE, NONE, NONE, 32648, NONE, 24424, 12178),
        (0, 90, 90, 54, 69, 69, 54, 54, 18),
        (0, 126, 118, 90, 90, 90, 90, 85, 54),
        (1, 30078, 90970, 135770, 90970, 90970, 11574, 11574, 30006),
        (1, 72538, 28022, 11574, 15429, 74265, 90970, 78120, 219666),
        (1, 70996, 5920, 76064, 72209, 5920, 76064, 16971, 72466),
        (1, 3864, NONE, 7976, NONE, NONE, 26480, NONE, 78120),
        (0, 91, 91, 39, 39, 70, 46, 38, 19),
        (0, 110, 126, 91, 91, 91, 84, 86, 46),
        (1, 140910, 91227, 91227, 136027, 91227, 221208, 7462, 27950),
        (1, 225320, 30078, 225320, 225320, 219152, 78120, 224806, 229432),
        (1, 72795, 229432, 134485, 133714, 7719, 9518, 17228, 70410),
        (1, 5920, 133457, 15686, 7719, 133971, 133971, 89171, 132172),
        (1, NONE, NONE, 78120, NONE, NONE, NONE, 133971, NONE),
        (0, 1, 1, 0, 0, 1, 1, 1, 96),
        (0, 146, 144, 136, 120, 127, 136, 96, 148),
        (1, 86930, NONE, NONE, NONE, NONE, NONE, NONE, 8084),
        (0, 25, 31, 38, 25, 33, 62, 68, 20),
        (0, 118, 92, 92, 46, 46, 85, 87, 62),
        (1, 28022, 136284, 68611, 74265, 226862, 32648, 17485, 70924),
        (1, 15943, 87372, 7719, 9518, 9775, 89171, 231488, 231488),
        (1, 227376, 7976, 227376, 133971, 76321, 227119, 134228, 132429),
        (1, 135770, 231231, 136027, NONE, 221208, 135770, NONE, NONE),
        (1, NONE, 133714, NONE, NONE, 135770, NONE, NONE, NONE),
        (0, 2, 2, 1, 1, 2, 2, 2, 104),
        (0, 88, 88, 119, 128, 112, 135, 120, 147),
        (1, 72024, NONE, NONE, NONE, NONE, NONE, NONE, 10131),
        (0, 33, 25, 46, 33, 34, 31, 25, 11),
        (0, 102, 39, 93, 54, 54, 86, 69, 31),
        (1, NONE, 74265, 7462, 228918, 15429, 13630, 74265, 223007),
        (1, NONE, 15686, NONE, 76321, 76578, NONE, 17742, 71181),
        (1, NONE, 69125, NONE, 78120, NONE, NONE, NONE, NONE),
        (0, 41, 33, 17, 62, 61, 55, 33, 14),
        (0, 119, 67, 66, 92, 84, 87, 70, 89),
        (1, 229432, 76321, 72209, 13630, 223264, 225063, 76321, 15961),
        (1, 16714, 227119, 229175, 229175, 136027, 32391, 233544, 233544),
        (1, 145022, 135770, 136284, 134228, 15686, 134228, 18256, 72723),
        (1, NONE, 15943, 9518, NONE, 87372, NONE, 134485, 132686),
        (0, 3, 4, 2, 3, 3, 3, 3, 112),
        (0, 144, 96, 144, 136, 120, 104, 128, 145),
        (1, 86416, NONE, NONE, NONE, NONE, NONE, NONE, 14225),
        (0, 99, 86, 99, 38, 62, 91, 18, 45),
        (0, 117, 117, 109, 99, 99, 127, 45, 82),
        (1, 142709, 27765, 16971, 7462, 93283, 80176, 226605, 27693),
        (1, 16971, 5663, 231231, 16971, 11574, 30335, 72466, 72980),
        (1, 221465, 80176, 136541, 231231, 231231, 228918, 22368, 22296),
        (1, 136027, 229175, NONE, 135770, 134228, 134485, 219152, 231231),
        (1, NONE, 136027, NONE, NONE, NONE, NONE, 134742, 132943),
        (0, 4, 0, 4, 4, 4, 4, 4, 0),
        (0, 96, 104, 88, 144, 128, 120, 135, 90),
        (1, 74080, NONE, NONE, NONE, NONE, NONE, NONE, 16128),
        (0, 100, 68, 25, 45, 68, 33, 26, 27),
        (0, 109, 93, 117, 100, 85, 67, 30, 95),
        (1, 69454, 68097, 74265, 226605, 78120, 76321, 74522, 88914),
        (1, 1808, 7719, 17228, 17228, 13373, 5920, 15172, 24352),
        (1, NONE, NONE, NONE, NONE, NONE, 82232, NONE, NONE),
        (0, 47, 100, 33, 41, 31, 26, 27, 38),
        (0, 49, 109, 68, 68, 86, 68, 61, 83),
        (1, 9775, 223007, 76321, 78377, 225063, 74522, 74779, 229175),
        (1, 223521, 16714, 228918, 227119, 82232, 223007, 227119, 74779),
        (1, 74851, 68354, 138083, 136284, 138083, 7976, 28536, 24095),
        (1, 24167, 134742, 3864, 3864, 13630, 87886, 80176, 155974),
        (1, 142966, NONE, NONE, NONE, NONE, 134742, 134999, NONE),
        (0, 5, 11, 5, 5, 5, 5, 5, 120),
        (0, 104, 112, 96, 96, 118, 128, 111, 151),
        (1, 76136, NONE, NONE, NONE, NONE, NONE, NONE, NONE),
        (0, 26, 69, 41, 23, 26, 41, 41, 25),
        (0, 31, 84, 69, 26, 38, 69, 62, 29),
        (1, 75108, 89428, 78377, 74522, 74522, 16971, 82232, 89171),
        (1, 26223, 17228, 28279, 5920, 16971, 89428, 15429, 25894),
        (1, 225577, 68868, 225063, 225063, 87629, 134999, 222750, 218124),
        (1, 138854, 225063, 140653, 138083, 227119, NONE, NONE, 156222),
        (1, NONE, NONE, NONE, NONE, 134485, NONE, NONE, NONE),
        (0, 6, NONE, 9, 6, 6, 6, 6, 103),
        (0, 89, NONE, 104, 126, 144, 144, 110, 150),
        (1, 72281, 142709, NONE, NONE, NONE, NONE, NONE, NONE),
        (0, 34, 13, 23, 31, 41, 23, 49, 21),
        (0, 39, 120, 26, 34, 60, 49, 103, 66),
        (1, 25966, NONE, 74522, 76578, 30335, 220951, 15686, 1943),
        (1, NONE, NONE, NONE, NONE, 87886, 17228, 88143, 74265),
        (1, NONE, NONE, NONE, NONE, NONE, 89685, NONE, NONE),
        (0, 42, 15, NONE, NONE, 30, 30, 19, 28),
        (0, 108, 41, NONE, NONE, 49, 92, 37, 67),
        (1, 227633, 70667, 14658, 80176, 228918, 222750, 224549, 218381),
        (1, 138083, 1808, NONE, 24424, 9518, 11831, 30592, 23581),
        (1, 28279, NONE, NONE, NONE, 88143, 91227, 89428, 80176),
        (1, NONE, NONE, NONE, NONE, 134742, 136027, NONE, 131401),
        (0, 38, 23, 34, 61, 7, 7, 7, 128),
        (0, 112, 49, 108, 108, 88, 96, 117, 149),
        (1, 78192, 218895, 76578, 226862, NONE, NONE, NONE, NONE),
        (0, 62, NONE, NONE, NONE, 37, 34, 21, 68),
        (0, 85, NONE, NONE, NONE, 92, 38, 127, 81),
        (1, 71253, 71181, 224806, 11574, 15172, 24424, 32391, 3990),
        (1, 27765, 136541, 15172, 138340, 89428, 78377, 89685, 82232),
        (1, 221722, 3864, 142709, 87629, 223007, 224806, 220437, 219923),
        (1, 138340, NONE, 80176, NONE, NONE, NONE, NONE, 137055),
        (0, 9, 3, 18, 19, 9, 9, 9, 2),
        (0, 120, 128, 112, 112, 96, 119, 136, 136),
        (1, 80248, NONE, NONE, NONE, NONE, NONE, NONE, NONE),
        (0, 14, 12, 31, 30, 42, 42, 22, 33),
        (0, 55, 62, 42, 42, 53, 60, 53, 69),
        (1, 5663, 14915, 78634, 78634, 89685, 80433, 78377, 70667),
        (1, NONE, NONE, NONE, NONE, 5663, 14915, 13373, 6037),
        (0, 63, NONE, NONE, NONE, 29, 27, 28, 41),
        (0, 93, NONE, NONE, NONE, 35, 61, 126, 71),
        (1, 73309, 78377, 15429, 15172, 224806, 221979, 220694, 220180),
        (1, 223778, 220951, 90970, 87886, 78377, 15172, 26223, 90970),
        (1, 140653, 138340, 226862, 220951, 28022, 91484, 80433, 16642),
        (1, 7719, NONE, 140396, 140396, NONE, NONE, NONE, NONE),
        (0, 12, 20, 10, 7, 10, 10, 10, 3),
        (0, 128, 135, 120, 117, 104, 111, 144, 144),
        (1, 82304, NONE, NONE, NONE, NONE, NONE, NONE, NONE),
        (0, 57, 26, 49, 29, 57, 35, 29, 26),
        (0, 87, 38, 61, 43, 66, 45, 118, 87),
        (1, 7462, 15172, 72466, 78891, 7462, 76578, 72723, 94311),
        (1, 225834, 80433, 3607, 30078, 80433, 15429, 13630, 16899),
        (1, 140396, NONE, NONE, 68354, 222750, 226605, 222236, 218638),
        (0, 45, 34, 50, 37, 11, 11, 11, 4),
        (0, 97, 65, 62, 85, 135, 126, 88, 135),
        (1, 74337, 15429, 220951, 223007, NONE, NONE, NONE, NONE),
        (1, NONE, 70924, 5663, 91227, NONE, NONE, NONE, NONE),
        (1, NONE, 140653, 80433, 5663, NONE, NONE, NONE, NONE),
        (0, 10, 6, 12, 9, 65, 36, 23, 15),
        (0, 95, 119, 127, 127, 67, 52, 91, 59),
        (1, 13630, NONE, NONE, NONE, 13116, 78634, 91227, 88657),
        (1, NONE, NONE, NONE, NONE, 91484, 13116, 25966, 17156),
        (0, 11, 42, 22, 35, 15, 53, 31, 36),
        (0, 94, 66, 35, 66, 87, 57, 36, 111),
        (1, 231488, 72980, 13373, 91484, 224549, 224292, 222493, 221979),
        (1, 11831, 1551, 80690, 13373, 78634, 74779, 24167, 76321),
        (1, NONE, NONE, 223007, 222750, NONE, NONE, NONE, NONE),
        (0, 18, 9, 13, 10, NONE, NONE, 12, 5),
        (0, 105, 127, 135, 135, NONE, NONE, 119, 127),
        (1, 76393, NONE, NONE, NONE, 5406, 13373, NONE, 17413),
        (0, 13, 7, 30, 49, 18, 18, 66, 37),
        (0, 101, 50, 43, 67, 111, 103, 92, 60),
        (1, 13887, 3607, 13630, 72723, NONE, NONE, 91484, 78377),
        (1, 218638, 74522, 76835, 5406, NONE, NONE, 27765, 224806),
        (1, NONE, NONE, NONE, NONE, NONE, NONE, 224292, NONE),
        (0, 54, 35, 51, 15, 23, 65, 13, 6),
        (0, 113, 94, 65, 65, 93, 66, 102, 84),
        (1, 78449, 76578, 222750, 224549, 11317, 76835, NONE, 17670),
        (1, NONE, NONE, 3350, 27765, NONE, NONE, NONE, NONE),
        (0, 7, NONE, NONE, NONE, NONE, NONE, 34, 49),
        (0, 20, NONE, NONE, NONE, NONE, NONE, 67, 61),
        (1, 9261, 13630, 78891, 89685, 76835, 11060, 76578, 74522),
        (0, 22, 10, 19, 11, 19, 12, NONE, 22),
        (0, 92, 103, 126, 119, 119, 95, NONE, 119),
        (1, NONE, NONE, NONE, NONE, NONE, NONE, 30335, 220437),
        (0, 19, 43, 52, 86, 94, 88, 46, 7),
        (0, 121, 102, 67, 110, 95, 118, 57, 85),
        (1, 80505, 7462, 5406, 5149, 5149, 11317, 11317, 17927),
        (1, NONE, 78634, 80947, 76835, NONE, NONE, NONE, NONE),
        (0, 15, 18, 20, 12, 45, 37, 14, 57),
        (0, 50, 111, 111, 111, 100, 93, 109, 126),
        (1, NONE, NONE, NONE, NONE, NONE, NONE, NONE, 222236),
        (0, 46, 51, 7, 57, 12, 13, 65, 91),
        (0, 98, 101, 57, 87, 126, 102, 95, 97),
        (1, 74594, 80690, 81204, 7205, NONE, NONE, 30078, 15713),
        (0, 23, 57, 15, 59, 50, 59, 15, 30),
        (0, 58, 110, 86, 88, 59, 94, 93, 52),
        (1, NONE, 76835, NONE, NONE, NONE, NONE, NONE, NONE),
        (0, 21, 19, 21, 18, 27, 14, 20, 65),
        (0, 65, 87, 110, 118, 103, 110, 58, 102),
        (0, 30, 99, 58, 60, 58, 22, NONE, 92),
        (0, 106, 108, 87, 93, 117, 50, NONE, 98),
        (1, 76650, 78891, NONE, NONE, NONE, NONE, 28022, 13666),
        (0, 29, 14, 27, 20, 22, 58, 59, 34),
        (0, 66, 95, 118, 95, 101, 109, 99, 53),
        (0, 27, 22, 11, 14, 13, 15, 94, 1),
        (0, 114, 27, 59, 94, 110, 99, 60, 86),
        (1, 78706, 80947, NONE, NONE, NONE, NONE, NONE, NONE),
        (0, 35, 30, 60, 22, 43, 28, 112, 42),
        (0, 67, 58, 100, 50, 52, 29, 100, 101),
        (0, 43, 45, 37, 27, 14, 19, 51, 50),
        (0, 68, 29, 95, 103, 102, 117, 90, 94),
        (0, 28, 59, 6, 52, 21, 51, 42, 23),
        (0, 136, 21, 101, 58, 51, 100, 52, 99),
        (0, 51, 44, 45, 28, 36, 21, 101, 58),
        (0, 69, 53, 103, 102, 108, 101, 43, 108),
        (0, 37, 46, 14, 53, 109, 108, 50, 110),
        (0, 86, 52, 28, 101, 20, 43, 108, 35),
        (0, 59, 28, 53, 13, 44, 44, 35, 118),
        (0, 70, 54, 94, 51, 28, 20, 44, 43),
        (0, 44, 60, 36, 36, NONE, NONE, NONE, 44),
        (0, 61, 37, 102, 109, NONE, NONE, NONE, 93),
        (0, 36, 36, 29, 21, NONE, NONE, NONE, 51),
        (0, 52, 61, 44, 44, NONE, NONE, NONE, 117),
        (0, 53, NONE, NONE, NONE, NONE, NONE, NONE, 100),
        (0, 60, NONE, NONE, NONE, NONE, NONE, NONE, 109),
    ),
    (
        (1, 16200, 14144, 14144, 86344, 86344, 86344, 86344, 32576),
        (1, 67912, 86344, 86344, 16200, 16200, 16200, 16200, 86344),
        (1, 131144, 132429, 131915, 131658, 131144, 131144, 131144, 168504),
        (1, 69968, 16200, 16200, 14144, 12088, 14144, 12088, 34632),
        (1, 12088, 86601, 86601, 86601, 86601, 86601, 86601, 86601),
        (1, 131401, 131401, 131144, 131144, 131401, 131401, 131401, 169000),
        (1, 68169, 86858, 86858, 86858, 10032, 86858, 14144, 18184),
        (1, 14144, 18256, 17999, 18256, 86858, 18256, 71952, 69896),
        (1, 68683, 69896, 87372, 10032, 87115, 10032, 10032, 26408),
        (1, 17999, 12088, 18256, 87115, 17999, 69896, 69896, 86858),
        (1, 131658, 131658, 131401, 131401, 131658, 131658, 131658, 168752),
        (1, 68940, 87115, 12088, 12088, 18256, 12088, 86858, 28464),
        (1, 18256, 17999, 69896, 87372, 69896, 71952, 17999, 87115),
        (1, 131915, 132172, 131658, 131915, 131915, 131915, 131915, 168256),
        (1, 132172, 10032, 17742, 17742, 132172, 132172, 87115, 87372),
        (1, 7976, 131144, 10032, 17999, 71952, 17485, 132172, 87629),
        (1, 132429, 71952, 132172, 132172, 132429, 74008, 87372, 131144),
        (1, 68426, 74008, 132429, 132429, 7976, 132429, 132429, 87886),
        (1, 10032, NONE, 71952, NONE, 74008, 17742, 7976, 169744),
        (1, NONE, NONE, NONE, NONE, NONE, NONE, 87629, 71952),
        (0, 81, 63, 55, 55, 63, 63, 63, 9),
        (0, 127, 81, 81, 81, 81, 81, 81, 63),
        (1, 70225, 13887, 88657, 88657, 13887, 13887, 13887, 32319),
        (1, 30335, 88657, 11831, 11831, 88657, 88657, 88657, 74008),
        (1, 17228, 16971, 74008, 69896, 14144, 87115, 87886, 30520),
        (1, 69197, 76064, 133457, 132686, 132686, 17999, 22792, 169496),
        (1, 132686, NONE, NONE, NONE, NONE, 132686, 132686, NONE),
        (0, 82, 47, 63, 63, 55, 47, 55, 17),
        (0, 135, 82, 82, 82, 82, 82, 82, 47),
        (1, 70482, 88914, 88914, 88914, 11831, 9775, 11831, 28207),
        (1, 32391, 9775, 13887, 13887, 88914, 88914, 88914, 70153),
        (1, NONE, 131915, 87629, NONE, 132943, 132943, 132943, 169248),
        (0, 71, 55, 71, 70, 71, 25, 17, 10),
        (0, 83, 83, 83, 83, 83, 39, 71, 55),
        (1, 70739, 133971, 89171, 89171, 15943, 74265, 15943, 30263),
        (1, 17485, 11831, 15943, 15686, 89171, 7719, 74008, 72209),
        (1, NONE, NONE, NONE, 17485, 17228, 87372, NONE, NONE),
        (1, NONE, NONE, NONE, 71952, NONE, NONE, NONE, NONE),
        (0, 17, 70, 47, 71, 17, 17, 39, 12),
        (0, 103, 85, 84, 84, 39, 70, 83, 39),
        (1, 133457, 134485, 9775, 89428, 17485, 15686, 72209, 26151),
        (1, NONE, 17485, 89428, 15943, 76064, 87629, 133457, 131658),
        (1, NONE, 78120, 17485, 74008, 133457, 133457, NONE, NONE),
        (1, NONE, NONE, 133714, 7976, NONE, NONE, NONE, NONE),
        (1, NONE, NONE, NONE, 132943, NONE, NONE, NONE, NONE),
        (0, 84, 17, 70, 17, 25, 71, 47, 13),
        (0, 111, 71, 85, 47, 47, 83, 84, 70),
        (1, 17742, 17742, 87115, 9775, 17742, 15943, 9775, 76064),
        (1, 134228, 72209, 5920, 76064, 72209, 72209, 76064, 131915),
        (1, NONE, 132686, 134228, 133457, 133714, 133714, 133714, NONE),
        (0, 145, 136, 128, 104, 136, 112, 104, 88),
        (1, 86673, NONE, NONE, NONE, 32648, NONE, 24424, NONE),
        (0, 90, 90, 54, 69, 69, 54, 54, 18),
        (0, 126, 118, 90, 90, 90, 90, 85, 54),
        (1, 30078, 90970, 135770, 90970, 90970, 11574, 11574, 30006),
        (1, 72538, 28022, 11574, 15429, 74265, 90970, 78120, 72466),
        (1, 70996, 5920, 76064, 72209, 5920, 76064, 16971, 78120),
        (1, 3864, NONE, 7976, NONE, NONE, 26480, NONE, NONE),
        (0, 91, 91, 39, 39, 70, 46, 38, 19),
        (0, 110, 126, 91, 91, 91, 84, 86, 46),
        (1, 140910, 91227, 91227, 136027, 91227, 78120, 7462, 27950),
        (1, 72795, 30078, 15686, 7719, 7719, 9518, 17228, 70410),
        (1, 5920, 133457, 78120, 133714, 133971, 133971, 89171, 132172),
        (1, NONE, NONE, 134485, NONE, NONE, NONE, 133971, NONE),
        (0, 146, 144, 136, 120, 127, 136, 96, 96),
        (1, 86930, NONE, NONE, NONE, NONE, NONE, NONE, NONE),
        (0, 25, 31, 38, 25, 33, 62, 68, 20),
        (0, 118, 92, 92, 46, 46, 85, 87, 62),
        (1, 28022, 136284, 7719, 74265, 9775, 32648, 17485, 70924),
        (2,),
        (1, 15943, 87372, 229432, 9518, 76321, 89171, 223264, 219152),
        (1, 233801, 7976, NONE, 223264, 231488, 225320, NONE, NONE),
        (1, NONE, 231488, NONE, NONE, NONE, NONE, NONE, NONE),
        (0, 0, 5, 3, 2, 0, 0, 0, 146),
        (1, 135770, 133714, 68611, 133971, 135770, 135770, 134228, 12178),
        (1, NONE, NONE, 136027, NONE, NONE, NONE, NONE, 132429),
        (0, 88, 88, 119, 128, 112, 135, 120, 104),
        (1, 72024, NONE, NONE, NONE, NONE, NONE, NONE, NONE),
        (0, 33, 25, 46, 33, 34, 31, 25, 11),
        (0, 102, 39, 93, 54, 54, 86, 69, 31),
        (1, NONE, 74265, 7462, 76321, 15429, 13630, 74265, 71181),
        (1, NONE, 15686, NONE, 78120, 76578, NONE, 17742, NONE),
        (0, 41, 33, 17, 62, 61, 55, 33, 14),
        (0, 119, 67, 66, 92, 84, 87, 70, 89),
        (1, 234058, 76321, 72209, 13630, 229175, 231488, 76321, 15961),
        (1, NONE, 233544, 231488, 227376, NONE, NONE, 221208, 221208),
        (0, 1, 1, 0, 0, 1, 1, 1, 148),
        (1, 16714, 68097, 9518, 134228, 15686, 32391, 18256, 8084),
        (1, 145022, 15943, 136284, NONE, 87372, 134228, 134485, 72723),
        (1, NONE, 135770, NONE, NONE, 136027, NONE, NONE, 132686),
        (0, 144, 96, 144, 136, 120, 104, 128, 112),
        (1, 86416, NONE, NONE, NONE, NONE, NONE, NONE, NONE),
        (0, 99, 86, 99, 38, 62, 91, 18, 45),
        (0, 117, 117, 109, 99, 99, 127, 45, 82),
        (1, 142709, 27765, 16971, 7462, 93283, 80176, 72466, 27693),
        (1, 16971, 5663, 227119, 16971, 11574, 30335, 22368, 72980),
        (1, 219152, 80176, NONE, 229432, 225320, 231231, 227376, 22296),
        (1, NONE, 219152, NONE, NONE, NONE, NONE, NONE, 223264),
        (0, 2, 2, 1, 1, 2, 2, 2, 147),
        (1, 136027, 136027, 136541, 135770, 134228, 134485, 134742, 10131),
        (1, NONE, NONE, NONE, NONE, NONE, NONE, NONE, 132943),
        (0, 96, 104, 88, 144, 128, 120, 135, 90),
        (1, 74080, NONE, NONE, NONE, NONE, NONE, NONE, NONE),
        (0, 100, 68, 25, 45, 68, 33, 26, 27),
        (0, 109, 93, 117, 100, 85, 67, 30, 95),
        (1, 69454, 7719, 74265, 17228, 78120, 76321, 74522, 88914),
        (1, 1808, 68354, 17228, NONE, 13373, 5920, 15172, 24352),
        (1, NONE, NONE, NONE, NONE, NONE, 82232, NONE, NONE),
        (0, 47, 100, 33, 41, 31, 26, 27, 38),
        (1, 9775, NONE, NONE, NONE, NONE, NONE, NONE, NONE),
        (0, 49, 109, 68, 68, 86, 68, 61, 83),
        (1, 233544, 221208, 76321, 78377, 227376, 74522, 74779, 225320),
        (1, NONE, NONE, 233544, 231488, NONE, 223264, 229432, NONE),
        (0, 3, 4, 2, 3, 3, 3, 3, 145),
        (1, 74851, 16714, 3864, 3864, 82232, 7976, 28536, 14225),
        (1, 24167, 68868, 138083, 136284, 13630, 87886, 80176, 74779),
        (1, 142966, 134742, NONE, NONE, 138083, 134742, 134999, 24095),
        (1, NONE, NONE, NONE, NONE, NONE, NONE, NONE, 155974),
        (0, 104, 112, 96, 96, 118, 128, 111, 120),
        (1, 76136, NONE, NONE, NONE, NONE, NONE, NONE, NONE),
        (0, 26, 69, 41, 23, 26, 41, 41, 25),
        (0, 31, 84, 69, 26, 38, 69, 62, 29),
        (1, 75108, 89428, 78377, 74522, 74522, 16971, 82232, 89171),
        (1, 26223, 17228, 28279, 5920, 16971, 89428, 15429, 25894),
        (1, 221208, 69125, 219152, 233544, 87629, 227376, 231231, 219666),
        (1, NONE, NONE, NONE, NONE, 229432, NONE, NONE, NONE),
        (0, 4, NONE, 4, 4, 4, 4, 4, 0),
        (1, 138854, 223264, 140653, 138083, 134485, 134999, NONE, 156222),
        (0, 89, 0, 104, 126, 144, 144, 110, 103),
        (1, 72281, 142709, NONE, NONE, NONE, NONE, NONE, NONE),
        (0, 34, 120, 23, 31, 41, 23, 49, 21),
        (0, NONE, NONE, NONE, NONE, 60, 49, 103, 66),
        (1, 25966, NONE, NONE, NONE, 30335, 17228, 15686, 74265),
        (1, NONE, NONE, NONE, NONE, 87886, 89685, 88143, 16128),
        (0, 42, 15, 26, 34, 30, 30, 19, 28),
        (0, 108, 41, NONE, NONE, 49, 92, 37, 67),
        (1, 223264, 1808, 74522, 76578, 226862, 229432, 225063, 227376),
        (0, 5, 23, NONE, NONE, 5, 5, 5, 151),
        (1, 28279, NONE, 14658, 80176, 9518, 11831, 30592, 23581),
        (1, 138083, NONE, NONE, 24424, 88143, 91227, 89428, 80176),
        (0, 112, 49, 34, 61, NONE, NONE, NONE, NONE),
        (0, NONE, NONE, 108, 108, NONE, NONE, NONE, NONE),
        (1, 78192, 225320, 76578, 221208, 134742, 136027, NONE, 131401),
        (1, NONE, NONE, 221208, NONE, NONE, NONE, NONE, NONE),
        (0, 62, 11, 5, 5, 88, 96, 117, 128),
        (0, 85, NONE, NONE, NONE, 37, 34, 21, 68),
        (0, NONE, NONE, NONE, NONE, 92, 38, 127, 81),
        (1, 71253, 70667, 15172, 11574, 15172, 24424, 32391, 82232),
        (1, 27765, 3864, 80176, 87629, 89428, 78377, 89685, 1943),
        (1, 219409, 136541, 142709, 138340, 233544, 233544, 224806, 223007),
        (0, 6, 128, 112, 112, 6, 6, 6, 150),
        (1, NONE, NONE, NONE, NONE, NONE, NONE, NONE, 137055),
        (0, 10, 12, 31, 30, 96, 119, 136, 136),
        (0, 39, NONE, 42, 42, 42, 42, 22, 33),
        (1, 138340, 70924, 78634, 78634, NONE, NONE, NONE, NONE),
        (0, 120, 62, NONE, NONE, 53, 60, 53, 69),
        (1, 80248, 14915, 15429, 15172, 89685, 80433, 78377, 70667),
        (1, 5663, 78377, 90970, 87886, 5663, 14915, 13373, 3990),
        (0, 55, NONE, NONE, NONE, 29, 27, 28, 41),
        (0, 93, NONE, NONE, NONE, 35, 61, 126, 71),
        (1, 73309, 227376, 223264, 228918, 219152, 221208, 226605, 229432),
        (1, 225320, NONE, NONE, NONE, NONE, NONE, NONE, NONE),
        (0, 38, 13, 9, 6, 7, 7, 7, 149),
        (1, 7462, NONE, 140396, 140396, 78377, 15172, 26223, 90970),
        (1, 140653, NONE, NONE, NONE, 28022, 91484, 80433, 6037),
        (0, 128, 38, 120, 117, 104, 111, 144, 144),
        (1, 82304, 138340, NONE, NONE, NONE, NONE, NONE, NONE),
        (0, 57, 135, 49, 29, 57, 35, 29, 26),
        (0, 87, 26, 61, 43, 66, 45, 118, 87),
        (1, 7719, 15172, 3607, 78891, 7462, 76578, 72723, 94311),
        (1, 227376, 80433, NONE, 30078, 80433, 15429, 13630, 231488),
        (1, NONE, NONE, NONE, 68354, 221208, 227119, 231488, NONE),
        (0, 9, 34, 50, 37, 9, 9, 9, 2),
        (0, 11, 65, 62, 85, NONE, NONE, NONE, NONE),
        (1, 140396, 229432, 225320, 225320, NONE, NONE, NONE, 16642),
        (0, 97, 3, 18, 19, 135, 126, 88, 135),
        (1, 74337, 15429, 72466, 91227, NONE, NONE, NONE, NONE),
        (1, NONE, NONE, 5663, 5663, NONE, NONE, NONE, NONE),
        (0, 95, NONE, NONE, NONE, 65, 36, 23, 15),
        (1, 13630, 71181, 80433, NONE, NONE, NONE, NONE, NONE),
        (0, 13, NONE, 127, 127, 67, 52, 91, 59),
        (0, 94, NONE, 22, 35, NONE, NONE, NONE, NONE),
        (1, 229432, 140653, NONE, NONE, 13116, 78634, 91227, 88657),
        (0, 12, 119, 35, 66, NONE, NONE, NONE, NONE),
        (0, 105, 42, NONE, NONE, NONE, NONE, NONE, NONE),
        (1, 76393, NONE, 13373, 91484, 91484, 13116, 25966, NONE),
        (0, 14, 66, NONE, NONE, 15, 53, 31, 36),
        (0, 101, NONE, NONE, NONE, 87, 57, 36, 111),
        (1, 11831, 1551, 80690, 13373, 223264, 225063, 233544, 233544),
        (1, 221465, 231231, 227376, 226605, NONE, NONE, NONE, NONE),
        (0, 45, 20, 10, 7, 10, 10, 10, 3),
        (1, 9261, 72980, NONE, NONE, 78634, 74779, 24167, 16899),
        (1, NONE, NONE, NONE, NONE, 5406, 13373, NONE, 76321),
        (0, 20, 127, 135, 135, 111, 103, 119, 127),
        (0, 63, 7, 30, 49, 23, 65, 66, 37),
        (0, 113, 50, 43, 67, 93, 66, 92, 60),
        (1, 78449, 3607, 13630, 5406, 11317, 76835, 91484, 78377),
        (1, 13887, 74522, 76835, 72723, 76835, 11060, 27765, 231231),
        (0, 21, 35, 51, 15, NONE, NONE, NONE, 4),
        (0, 92, 94, 65, 65, NONE, NONE, NONE, NONE),
        (1, 223521, 227119, 229175, 229175, 231231, 228918, 219152, 17156),
        (0, 18, 6, 12, 9, 11, 11, 11, 84),
        (0, 121, NONE, NONE, NONE, 119, 95, 102, 49),
        (0, NONE, NONE, NONE, NONE, 94, 88, 34, 61),
        (1, 80505, 76578, 3350, 27765, NONE, NONE, NONE, 74522),
        (0, 7, NONE, NONE, NONE, 95, 118, 67, 22),
        (0, 50, NONE, NONE, NONE, NONE, NONE, NONE, 119),
        (1, 225577, 13630, 78891, 89685, 5149, 11317, 76578, 229175),
        (0, 54, 103, 126, 119, 45, 37, NONE, 5),
        (1, NONE, NONE, NONE, NONE, NONE, NONE, 30335, 17413),
        (0, 15, 43, 52, 86, 100, 93, 46, 85),
        (0, 98, 102, 67, 110, NONE, NONE, 57, 57),
        (1, 74594, 78634, 5406, 5149, NONE, NONE, NONE, NONE),
        (1, NONE, 7462, 80947, 76835, NONE, NONE, NONE, NONE),
        (0, NONE, NONE, NONE, NONE, NONE, NONE, NONE, 126),
        (1, NONE, 229175, 231231, 231231, 225063, 223007, 227119, 218124),
        (0, 58, 9, 13, 10, 18, 18, 12, 6),
        (1, NONE, NONE, NONE, NONE, NONE, NONE, 11317, 17670),
        (0, 22, 111, 111, 111, 126, 102, 109, 91),
        (0, 23, 51, 7, 57, 50, 59, 65, 30),
        (0, NONE, 101, 57, 87, 59, 94, 95, 52),
        (1, 227633, 80690, 81204, 7205, NONE, NONE, NONE, NONE),
        (0, 19, 57, 15, 59, NONE, NONE, NONE, 65),
        (0, 106, 110, 86, 88, NONE, NONE, NONE, 102),
        (1, 76650, 223007, 228918, 227119, 227119, 220951, 30078, 218381),
        (0, 29, 10, 19, 11, 19, 12, NONE, 7),
        (0, 65, NONE, 110, 118, NONE, NONE, NONE, NONE),
        (1, 221722, 76835, NONE, NONE, NONE, NONE, 222750, 17927),
        (0, 46, 87, 58, 60, 103, 110, 13, 92),
        (0, 66, 99, 87, 93, 58, 22, 93, 34),
        (0, 114, 108, NONE, NONE, 117, 50, 20, 53),
        (1, 78706, 78891, 225063, 225063, NONE, NONE, NONE, 219923),
        (1, NONE, 225063, NONE, NONE, NONE, NONE, NONE, NONE),
        (0, 35, 18, 20, 12, 22, 58, 58, 97),
        (1, NONE, NONE, NONE, NONE, NONE, NONE, 28022, 15713),
        (0, 67, 22, 11, 95, 101, 109, 59, 86),
        (0, 43, 27, 118, 14, NONE, NONE, 99, 42),
        (0, NONE, 95, 59, 94, NONE, NONE, NONE, 101),
        (1, 223778, 80947, NONE, NONE, NONE, NONE, NONE, NONE),
        (0, 30, 29, 60, 22, NONE, NONE, NONE, 50),
        (0, 136, 58, 100, 50, NONE, NONE, NONE, 94),
        (1, NONE, 218895, 224806, 226862, 228918, 222750, 224549, 220180),
        (0, 68, 19, 21, 18, 12, 13, 14, 98),
        (1, NONE, NONE, NONE, NONE, NONE, NONE, NONE, 13666),
        (0, 51, 30, 95, 103, 110, 99, 94, 99),
        (0, NONE, 59, 6, 52, 43, 28, 60, 58),
        (0, NONE, NONE, 101, 58, 52, 29, 112, 108),
        (1, 225834, 220951, 226862, 220951, 223007, 224806, 220437, 218638),
        (0, 27, 14, 27, 20, 27, 14, 15, 1),
        (0, 69, 44, 28, 102, 102, 117, 100, 110),
        (0, 86, 53, 103, 53, 21, 51, 51, 35),
        (0, 59, 36, 14, 101, 51, 100, 90, 118),
        (0, 61, 52, 53, 13, 36, 21, 42, 43),
        (0, 44, 45, 94, 51, 108, 101, 52, 44),
        (1, 231488, NONE, 220951, 223007, 224806, 221979, 220694, 221979),
        (0, 28, 46, 37, 27, 13, 15, 101, 23),
        (0, 70, 60, 102, 109, 109, 108, 43, 93),
        (0, 52, 21, 29, 21, 20, 43, 50, 51),
        (0, NONE, NONE, 44, 44, NONE, NONE, NONE, NONE),
        (1, 218638, NONE, 223007, 222750, NONE, NONE, 222236, NONE),
        (0, 37, 54, 45, 28, 44, 44, 108, 117),
        (1, NONE, NONE, 222750, 224549, 222750, 226605, NONE, 224806),
        (0, 53, 61, 36, 36, 14, 19, 35, 100),
        (0, 60, 28, NONE, NONE, 28, 20, 44, 109),
        (1, NONE, NONE, NONE, NONE, 224549, 224292, 222493, 220437),
        (0, 36, 37, NONE, NONE, NONE, NONE, NONE, NONE),
        (1, NONE, NONE, NONE, NONE, NONE, NONE, 224292, 222236),
    ),
)
OWN = BAND * HALF


def device_of(row, cols):
    return row // cols, lax.rem(row, cols)


def kernel(cols_hbm, blocks_hbm, out_ref, cols_ref, blocks_ref, own, square, upper, flipped, newband, in_sem, entered, send_sem, recv_sem):
    size = blocks_ref.shape[-1]
    loads = [
        pltpu.make_async_copy(cols_hbm, cols_ref, in_sem.at[0]),
        pltpu.make_async_copy(blocks_hbm, blocks_ref, in_sem.at[1]),
    ]
    for load in loads:
        load.start()
    cols = lax.axis_size("col")
    count = cols * lax.axis_size("row")
    me = lax.axis_index("row") * cols + lax.axis_index("col")
    place = lax.rem(me, RING)
    start = me - place
    targets = (
        start + lax.rem(place + 1, RING),
        start + lax.rem(place + RING - 1, RING),
        lax.rem(me + RING, count),
        lax.rem(me + count - RING, count),
    )
    barrier = pltpu.get_barrier_semaphore()
    peers = [device_of(target, cols) for target in targets]
    for peer in (peers[0], peers[1], peers[3]):
        pl.semaphore_signal(barrier, inc=1, device_id=peer, device_id_type=MESH)

    bits = [lax.rem(place // 2**n, 2) == 1 for n in range(3)]

    def pick(values):
        for bit in bits:
            values = [jnp.where(bit, high, low) for low, high in zip(values[::2], values[1::2])]
        return values[0]

    for load in loads:
        load.wait()
    missing = jnp.int32(0)
    for s in range(WINDOW - 1):
        offset = lax.rem(cols_ref[0, s] - me + BAND + count, count)
        missing += jnp.where(offset == s, 1, 0)

    for o in range(WINDOW):
        first = blocks_ref[0, min(o, WINDOW - 2)]
        second = blocks_ref[0, max(o - 1, 0)]
        block = jnp.where(o < missing, first, jnp.where(o == missing, jnp.zeros_like(first), second))
        own[:, o * size : (o + 1) * size] = block
        if o >= BAND:
            upper[OWN + o - BAND] = block
        else:
            slot = o * HALF + BAND - o
            upper[slot] = block.T
            flipped[slot] = block

    pl.semaphore_wait(barrier, 3)
    pl.semaphore_signal(entered, inc=1, device_id=peers[2], device_id_type=MESH)

    def copy(here, there, peer):
        return pltpu.make_async_remote_copy(
            src_ref=upper.at[here],
            dst_ref=upper.at[there],
            send_sem=send_sem,
            recv_sem=recv_sem.at[there],
            device_id=peer,
            device_id_type=MESH,
        )

    def send(code):
        direction = code >> 16
        ahead, far = (direction & 1) == 0, direction >= 2
        peer = tuple(
            jnp.where(far, jnp.where(ahead, c, d), jnp.where(ahead, a, b)) for a, b, c, d in zip(*peers)
        )
        copy(code & 255, (code >> 8) & 255, peer).start()

    def receive(here):
        copy(here, here, peers[0]).wait_recv()

    def turn(here):
        flipped[here] = upper[here].T

    def where_any(codes, code, action):
        if NONE in codes:
            pl.when(code != NONE)(functools.partial(action, code))
        else:
            action(code)

    def exchange(events):
        unturned, sending = [], False
        for kind, *codes in events:
            code = pick([jnp.int32(c) for c in codes]) if codes else None
            if kind == 1:
                where_any(codes, code, send)
            elif kind == 2:
                pl.semaphore_wait(entered, 1)
            else:
                if sending:
                    for late in unturned:
                        where_any(*late, turn)
                    unturned = []
                where_any(codes, code, receive)
                unturned.append((codes, code))
            sending = kind == 1
        for late in unturned:
            where_any(*late, turn)

    ring = lax.rem(me // RING, 16)
    ring = jnp.where((ring == 0) | (ring == 4), 1, 0)
    sends = jnp.int32(0)
    for n, events in enumerate(EVENTS):
        pl.when(ring == n)(functools.partial(exchange, events))
        counts = [sum(e[0] == 1 and e[1 + y] != NONE for e in events) for y in range(RING)]
        sends = jnp.where(ring == n, pick([jnp.int32(c) for c in counts]), sends)
    for d in range(HALF):
        flipped[OWN + d] = upper[OWN + d].T

    def block_at(k, j):
        if abs(k - j) > BAND:
            return jnp.zeros((size, size), upper.dtype)
        return upper[k * HALF + j - k] if k <= j else flipped[j * HALF + k - j]

    def product(factor, first, width):
        low, high = max(0, first - BAND), min(WINDOW, first + width + BAND)
        columns = [
            jnp.concatenate([block_at(k, j) for k in range(low, high)], axis=0) for j in range(first, first + width)
        ]
        return jnp.dot(
            factor[:, low * size : high * size],
            jnp.concatenate(columns, axis=1),
            preferred_element_type=jnp.float32,
        )

    for first in range(0, WINDOW, 2):
        width = min(2, WINDOW - first)
        total = product(own, first, width)
        for w in range(width):
            piece = total[:, w * size : (w + 1) * size]
            piece = jnp.where(missing == first + w, 0.0, piece).astype(square.dtype)
            square[:, (first + w) * size : (first + w + 1) * size] = piece
    for first in range(0, WINDOW, 2):
        width = min(2, WINDOW - first)
        total = product(square, first, width)
        for w in range(width):
            part = slice((first + w) * size, (first + w + 1) * size)
            value = 3.0 * square[:, part].astype(jnp.float32) - 2.0 * total[:, w * size : (w + 1) * size]
            newband[first + w] = value.astype(newband.dtype)
    for s in range(WINDOW - 1):
        out_ref[0, s] = jnp.where(s < missing, newband[s], newband[s + 1])

    for number in sorted({sum(e[0] == 1 and e[1 + y] != NONE for e in events) for events in EVENTS for y in range(RING)}):
        blocks = upper.at[pl.ds(0, number)]
        pl.when(sends == number)(lambda blocks=blocks: pltpu.make_async_copy(blocks, blocks, send_sem).wait())


def per_device(block_cols, blocks):
    size = blocks.shape[-1]
    kind = blocks.dtype
    return pl.pallas_call(
        kernel,
        out_shape=jax.ShapeDtypeStruct(blocks.shape, kind),
        in_specs=[pl.BlockSpec(memory_space=pltpu.HBM)] * 2,
        out_specs=pl.BlockSpec(memory_space=pltpu.VMEM),
        scratch_shapes=[
            pltpu.SMEM(block_cols.shape, block_cols.dtype),
            pltpu.VMEM(blocks.shape, kind),
            pltpu.VMEM((size, WINDOW * size), kind),
            pltpu.VMEM((size, WINDOW * size), kind),
            pltpu.VMEM((WINDOW * HALF, size, size), kind),
            pltpu.VMEM((WINDOW * HALF, size, size), kind),
            pltpu.VMEM((WINDOW, size, size), kind),
            pltpu.SemaphoreType.DMA((2,)),
            pltpu.SemaphoreType.REGULAR,
            pltpu.SemaphoreType.DMA,
            pltpu.SemaphoreType.DMA((WINDOW * HALF,)),
        ],
        compiler_params=pltpu.CompilerParams(collective_id=0, has_side_effects=True, vmem_limit_bytes=40 * 2**20),
        cost_estimate=pl.CostEstimate(flops=4 * 217 * size**3, bytes_accessed=2 * 2**20, transcendentals=0),
        name="purify",
    )(*(pltpu.with_memory_space_constraint(x, pltpu.HBM) for x in (block_cols, blocks)))


def solution(mesh):
    placed = (P(("row", "col"), None), P(("row", "col"), None, None, None))
    return jax.shard_map(
        per_device,
        mesh=mesh,
        in_specs=placed,
        out_specs=P(("row", "col"), None, None, None),
        check_vma=False,
    )
```

```python
import functools

import jax
import jax.numpy as jnp
from jax import lax
from jax.experimental import pallas as pl
from jax.experimental.pallas import tpu as pltpu
from jax.sharding import PartitionSpec as P

BAND = 8
WINDOW = 2 * BAND + 1
HALF = BAND + 1
RING = 8
MESH = pl.DeviceIdType.MESH

NONE = 2**18
EVENTS = (
    (
        (1, 16200, 14144, 14144, 86344, 86344, 86344, 86344, 168504),
        (1, 67912, 86344, 86344, 16200, 16200, 16200, 16200, 32576),
        (1, 131144, 132429, 131915, 131658, 131144, 131144, 131144, 86344),
        (1, 69968, 16200, 16200, 14144, 12088, 14144, 12088, 34632),
        (1, 12088, 86601, 86601, 86601, 86601, 86601, 86601, 86601),
        (1, 131401, 131401, 131144, 131144, 131401, 131401, 131401, 169000),
        (1, 68169, 86858, 86858, 86858, 10032, 86858, 14144, 18184),
        (1, 14144, 18256, 17999, 18256, 86858, 18256, 71952, 69896),
        (1, 131658, 131658, 131401, 10032, 131658, 10032, 10032, 26408),
        (1, 68683, 69896, 87372, 131401, 87115, 131658, 131658, 168752),
        (1, 17999, 12088, 18256, 87115, 17999, 69896, 69896, 86858),
        (1, 68940, 87115, 12088, 12088, 18256, 12088, 86858, 28464),
        (1, 18256, 17999, 69896, 87372, 69896, 71952, 17999, 87115),
        (2,),
        (1, 233801, 231488, 229432, 223264, 231488, 225320, 223264, 219152),
        (1, 131915, 132172, 131658, 131915, 131915, 131915, 131915, 168256),
        (1, 234058, 233544, 17742, 17742, 132172, 231488, 221208, 87372),
        (1, 132172, 131144, 231488, 227376, 71952, 132172, 87115, 221208),
        (1, 7976, 10032, 132172, 132172, 225320, 17485, 132172, 131144),
        (1, 219152, 71952, 10032, 17999, 132429, 74008, 87372, 87629),
        (1, 132429, 219152, 132429, 229432, 7976, 132429, 227376, 87886),
        (1, 68426, 74008, 71952, 132429, 74008, 17742, 132429, 223264),
        (1, 10032, NONE, NONE, NONE, NONE, NONE, 7976, 169744),
        (1, NONE, NONE, NONE, NONE, NONE, NONE, 87629, 71952),
        (0, 81, 63, 55, 55, 63, 63, 63, 9),
        (0, 127, 81, 81, 81, 81, 81, 81, 63),
        (1, 70225, 13887, 88657, 88657, 13887, 13887, 13887, 32319),
        (1, 30335, 88657, 11831, 11831, 88657, 88657, 88657, 225320),
        (1, 233544, 221208, 233544, 231488, 227376, 231231, 229432, 74008),
        (1, 17228, 16971, 133457, 132686, 14144, 223264, 87886, 169496),
        (1, 69197, 76064, 74008, 69896, 132686, 87115, 132686, 30520),
        (1, 132686, NONE, NONE, NONE, NONE, 132686, 22792, NONE),
        (1, NONE, NONE, NONE, NONE, NONE, 17999, NONE, NONE),
        (0, 82, 47, 63, 63, 55, 47, 55, 17),
        (0, 135, 82, 82, 82, 82, 82, 82, 47),
        (1, 70482, 88914, 88914, 88914, 229175, 9775, 11831, 28207),
        (1, 32391, 9775, 13887, 13887, 11831, 88914, 88914, 70153),
        (1, 221208, 223264, 87629, 233544, 88914, 227376, 231231, 169248),
        (1, NONE, 131915, 219152, NONE, 229432, 132943, 132943, NONE),
        (1, NONE, NONE, NONE, NONE, 132943, NONE, NONE, NONE),
        (0, 71, 55, 71, 70, 71, 25, 17, 10),
        (0, 83, 83, 83, 83, 83, 39, 71, 55),
        (1, 70739, 133971, 89171, 89171, 15943, 74265, 15943, 30263),
        (1, 17485, 11831, 15943, 15686, 89171, 7719, 74008, 72209),
        (1, NONE, NONE, NONE, 17485, 17228, 87372, NONE, NONE),
        (1, NONE, NONE, NONE, 71952, NONE, NONE, NONE, NONE),
        (0, 17, 70, 47, 71, 17, 17, 39, 12),
        (0, 103, 85, 84, 84, 39, 70, 83, 39),
        (1, 223264, 134485, 227119, 89428, 133457, 229432, 225063, 26151),
        (1, 133457, 225320, 9775, 15943, 17485, 133457, 133457, 227376),
        (1, NONE, 17485, 89428, 221208, 76064, 15686, 72209, 131658),
        (1, NONE, 78120, 221208, 132943, NONE, 87629, NONE, NONE),
        (1, NONE, NONE, 17485, 74008, NONE, NONE, NONE, NONE),
        (1, NONE, NONE, 133714, 7976, NONE, NONE, NONE, NONE),
        (0, 84, 17, 70, 17, 25, 71, 47, 13),
        (0, 111, 71, 85, 47, 47, 83, 84, 70),
        (1, 17742, 17742, 87115, 9775, 17742, 15943, 9775, 76064),
        (1, 219409, 72209, 5920, 76064, 72209, 72209, 76064, 131915),
        (1, 134228, 227376, 223264, 133457, 233544, 233544, 133714, NONE),
        (1, NONE, 132686, 134228, NONE, 133714, 133714, NONE, NONE),
        (0, 0, 5, 3, 2, 0, 0, 0, 88),
        (0, 145, 136, 128, 104, 136, 112, 104, 146),
        (1, 86673, NONE, NONE, NONE, 32648, NONE, 24424, 12178),
        (0, 90, 90, 54, 69, 69, 54, 54, 18),
        (0, 126, 118, 90, 90, 90, 90, 85, 54),
        (1, 30078, 90970, 135770, 90970, 90970, 11574, 11574, 30006),
        (1, 72538, 28022, 11574, 15429, 74265, 90970, 78120, 219666),
        (1, 70996, 5920, 76064, 72209, 5920, 76064, 16971, 72466),
        (1, 3864, NONE, 7976, NONE, NONE, 26480, NONE, 78120),
        (0, 91, 91, 39, 39, 70, 46, 38, 19),
        (0, 110, 126, 91, 91, 91, 84, 86, 46),
        (1, 140910, 91227, 91227, 136027, 91227, 221208, 7462, 27950),
        (1, 225320, 30078, 225320, 225320, 219152, 78120, 224806, 229432),
        (1, 72795, 229432, 134485, 133714, 7719, 9518, 17228, 70410),
        (1, 5920, 133457, 15686, 7719, 133971, 133971, 89171, 132172),
        (1, NONE, NONE, 78120, NONE, NONE, NONE, 133971, NONE),
        (0, 1, 1, 0, 0, 1, 1, 1, 96),
        (0, 146, 144, 136, 120, 127, 136, 96, 148),
        (1, 86930, NONE, NONE, NONE, NONE, NONE, NONE, 8084),
        (0, 25, 31, 38, 25, 33, 62, 68, 20),
        (0, 118, 92, 92, 46, 46, 85, 87, 62),
        (1, 28022, 136284, 68611, 74265, 226862, 32648, 17485, 70924),
        (1, 15943, 87372, 7719, 9518, 9775, 89171, 231488, 231488),
        (1, 227376, 7976, 227376, 133971, 76321, 227119, 134228, 132429),
        (1, 135770, 231231, 136027, NONE, 221208, 135770, NONE, NONE),
        (1, NONE, 133714, NONE, NONE, 135770, NONE, NONE, NONE),
        (0, 2, 2, 1, 1, 2, 2, 2, 104),
        (0, 88, 88, 119, 128, 112, 135, 120, 147),
        (1, 72024, NONE, NONE, NONE, NONE, NONE, NONE, 10131),
        (0, 33, 25, 46, 33, 34, 31, 25, 11),
        (0, 102, 39, 93, 54, 54, 86, 69, 31),
        (1, NONE, 74265, 7462, 228918, 15429, 13630, 74265, 223007),
        (1, NONE, 15686, NONE, 76321, 76578, NONE, 17742, 71181),
        (1, NONE, 69125, NONE, 78120, NONE, NONE, NONE, NONE),
        (0, 41, 33, 17, 62, 61, 55, 33, 14),
        (0, 119, 67, 66, 92, 84, 87, 70, 89),
        (1, 229432, 76321, 72209, 13630, 223264, 225063, 76321, 15961),
        (1, 16714, 227119, 229175, 229175, 136027, 32391, 233544, 233544),
        (1, 145022, 135770, 136284, 134228, 15686, 134228, 18256, 72723),
        (1, NONE, 15943, 9518, NONE, 87372, NONE, 134485, 132686),
        (0, 3, 4, 2, 3, 3, 3, 3, 112),
        (0, 144, 96, 144, 136, 120, 104, 128, 145),
        (1, 86416, NONE, NONE, NONE, NONE, NONE, NONE, 14225),
        (0, 99, 86, 99, 38, 62, 91, 18, 45),
        (0, 117, 117, 109, 99, 99, 127, 45, 82),
        (1, 142709, 27765, 16971, 7462, 93283, 80176, 226605, 27693),
        (1, 16971, 5663, 231231, 16971, 11574, 30335, 72466, 72980),
        (1, 221465, 80176, 136541, 231231, 231231, 228918, 22368, 22296),
        (1, 136027, 229175, NONE, 135770, 134228, 134485, 219152, 231231),
        (1, NONE, 136027, NONE, NONE, NONE, NONE, 134742, 132943),
        (0, 4, 0, 4, 4, 4, 4, 4, 0),
        (0, 96, 104, 88, 144, 128, 120, 135, 90),
        (1, 74080, NONE, NONE, NONE, NONE, NONE, NONE, 16128),
        (0, 100, 68, 25, 45, 68, 33, 26, 27),
        (0, 109, 93, 117, 100, 85, 67, 30, 95),
        (1, 69454, 68097, 74265, 226605, 78120, 76321, 74522, 88914),
        (1, 1808, 7719, 17228, 17228, 13373, 5920, 15172, 24352),
        (1, NONE, NONE, NONE, NONE, NONE, 82232, NONE, NONE),
        (0, 47, 100, 33, 41, 31, 26, 27, 38),
        (0, 49, 109, 68, 68, 86, 68, 61, 83),
        (1, 9775, 223007, 76321, 78377, 225063, 74522, 74779, 229175),
        (1, 223521, 16714, 228918, 227119, 82232, 223007, 227119, 74779),
        (1, 74851, 68354, 138083, 136284, 138083, 7976, 28536, 24095),
        (1, 24167, 134742, 3864, 3864, 13630, 87886, 80176, 155974),
        (1, 142966, NONE, NONE, NONE, NONE, 134742, 134999, NONE),
        (0, 5, 11, 5, 5, 5, 5, 5, 120),
        (0, 104, 112, 96, 96, 118, 128, 111, 151),
        (1, 76136, NONE, NONE, NONE, NONE, NONE, NONE, NONE),
        (0, 26, 69, 41, 23, 26, 41, 41, 25),
        (0, 31, 84, 69, 26, 38, 69, 62, 29),
        (1, 75108, 89428, 78377, 74522, 74522, 16971, 82232, 89171),
        (1, 26223, 17228, 28279, 5920, 16971, 89428, 15429, 25894),
        (1, 225577, 68868, 225063, 225063, 87629, 134999, 222750, 218124),
        (1, 138854, 225063, 140653, 138083, 227119, NONE, NONE, 156222),
        (1, NONE, NONE, NONE, NONE, 134485, NONE, NONE, NONE),
        (0, 6, NONE, 9, 6, 6, 6, 6, 103),
        (0, 89, NONE, 104, 126, 144, 144, 110, 150),
        (1, 72281, 142709, NONE, NONE, NONE, NONE, NONE, NONE),
        (0, 34, 13, 23, 31, 41, 23, 49, 21),
        (0, 39, 120, 26, 34, 60, 49, 103, 66),
        (1, 25966, NONE, 74522, 76578, 30335, 220951, 15686, 1943),
        (1, NONE, NONE, NONE, NONE, 87886, 17228, 88143, 74265),
        (1, NONE, NONE, NONE, NONE, NONE, 89685, NONE, NONE),
        (0, 42, 15, NONE, NONE, 30, 30, 19, 28),
        (0, 108, 41, NONE, NONE, 49, 92, 37, 67),
        (1, 227633, 70667, 14658, 80176, 228918, 222750, 224549, 218381),
        (1, 138083, 1808, NONE, 24424, 9518, 11831, 30592, 23581),
        (1, 28279, NONE, NONE, NONE, 88143, 91227, 89428, 80176),
        (1, NONE, NONE, NONE, NONE, 134742, 136027, NONE, 131401),
        (0, 38, 23, 34, 61, 7, 7, 7, 128),
        (0, 112, 49, 108, 108, 88, 96, 117, 149),
        (1, 78192, 218895, 76578, 226862, NONE, NONE, NONE, NONE),
        (0, 62, NONE, NONE, NONE, 37, 34, 21, 68),
        (0, 85, NONE, NONE, NONE, 92, 38, 127, 81),
        (1, 71253, 71181, 224806, 11574, 15172, 24424, 32391, 3990),
        (1, 27765, 136541, 15172, 138340, 89428, 78377, 89685, 82232),
        (1, 221722, 3864, 142709, 87629, 223007, 224806, 220437, 219923),
        (1, 138340, NONE, 80176, NONE, NONE, NONE, NONE, 137055),
        (0, 9, 3, 18, 19, 9, 9, 9, 2),
        (0, 120, 128, 112, 112, 96, 119, 136, 136),
        (1, 80248, NONE, NONE, NONE, NONE, NONE, NONE, NONE),
        (0, 14, 12, 31, 30, 42, 42, 22, 33),
        (0, 55, 62, 42, 42, 53, 60, 53, 69),
        (1, 5663, 14915, 78634, 78634, 89685, 80433, 78377, 70667),
        (1, NONE, NONE, NONE, NONE, 5663, 14915, 13373, 6037),
        (0, 63, NONE, NONE, NONE, 29, 27, 28, 41),
        (0, 93, NONE, NONE, NONE, 35, 61, 126, 71),
        (1, 73309, 78377, 15429, 15172, 224806, 221979, 220694, 220180),
        (1, 223778, 220951, 90970, 87886, 78377, 15172, 26223, 90970),
        (1, 140653, 138340, 226862, 220951, 28022, 91484, 80433, 16642),
        (1, 7719, NONE, 140396, 140396, NONE, NONE, NONE, NONE),
        (0, 12, 20, 10, 7, 10, 10, 10, 3),
        (0, 128, 135, 120, 117, 104, 111, 144, 144),
        (1, 82304, NONE, NONE, NONE, NONE, NONE, NONE, NONE),
        (0, 57, 26, 49, 29, 57, 35, 29, 26),
        (0, 87, 38, 61, 43, 66, 45, 118, 87),
        (1, 7462, 15172, 72466, 78891, 7462, 76578, 72723, 94311),
        (1, 225834, 80433, 3607, 30078, 80433, 15429, 13630, 16899),
        (1, 140396, NONE, NONE, 68354, 222750, 226605, 222236, 218638),
        (0, 45, 34, 50, 37, 11, 11, 11, 4),
        (0, 97, 65, 62, 85, 135, 126, 88, 135),
        (1, 74337, 15429, 220951, 223007, NONE, NONE, NONE, NONE),
        (1, NONE, 70924, 5663, 91227, NONE, NONE, NONE, NONE),
        (1, NONE, 140653, 80433, 5663, NONE, NONE, NONE, NONE),
        (0, 10, 6, 12, 9, 65, 36, 23, 15),
        (0, 95, 119, 127, 127, 67, 52, 91, 59),
        (1, 13630, NONE, NONE, NONE, 13116, 78634, 91227, 88657),
        (1, NONE, NONE, NONE, NONE, 91484, 13116, 25966, 17156),
        (0, 11, 42, 22, 35, 15, 53, 31, 36),
        (0, 94, 66, 35, 66, 87, 57, 36, 111),
        (1, 231488, 72980, 13373, 91484, 224549, 224292, 222493, 221979),
        (1, 11831, 1551, 80690, 13373, 78634, 74779, 24167, 76321),
        (1, NONE, NONE, 223007, 222750, NONE, NONE, NONE, NONE),
        (0, 18, 9, 13, 10, NONE, NONE, 12, 5),
        (0, 105, 127, 135, 135, NONE, NONE, 119, 127),
        (1, 76393, NONE, NONE, NONE, 5406, 13373, NONE, 17413),
        (0, 13, 7, 30, 49, 18, 18, 66, 37),
        (0, 101, 50, 43, 67, 111, 103, 92, 60),
        (1, 13887, 3607, 13630, 72723, NONE, NONE, 91484, 78377),
        (1, 218638, 74522, 76835, 5406, NONE, NONE, 27765, 224806),
        (1, NONE, NONE, NONE, NONE, NONE, NONE, 224292, NONE),
        (0, 54, 35, 51, 15, 23, 65, 13, 6),
        (0, 113, 94, 65, 65, 93, 66, 102, 84),
        (1, 78449, 76578, 222750, 224549, 11317, 76835, NONE, 17670),
        (1, NONE, NONE, 3350, 27765, NONE, NONE, NONE, NONE),
        (0, 7, NONE, NONE, NONE, NONE, NONE, 34, 49),
        (0, 20, NONE, NONE, NONE, NONE, NONE, 67, 61),
        (1, 9261, 13630, 78891, 89685, 76835, 11060, 76578, 74522),
        (0, 22, 10, 19, 11, 19, 12, NONE, 22),
        (0, 92, 103, 126, 119, 119, 95, NONE, 119),
        (1, NONE, NONE, NONE, NONE, NONE, NONE, 30335, 220437),
        (0, 19, 43, 52, 86, 94, 88, 46, 7),
        (0, 121, 102, 67, 110, 95, 118, 57, 85),
        (1, 80505, 7462, 5406, 5149, 5149, 11317, 11317, 17927),
        (1, NONE, 78634, 80947, 76835, NONE, NONE, NONE, NONE),
        (0, 15, 18, 20, 12, 45, 37, 14, 57),
        (0, 50, 111, 111, 111, 100, 93, 109, 126),
        (1, NONE, NONE, NONE, NONE, NONE, NONE, NONE, 222236),
        (0, 46, 51, 7, 57, 12, 13, 65, 91),
        (0, 98, 101, 57, 87, 126, 102, 95, 97),
        (1, 74594, 80690, 81204, 7205, NONE, NONE, 30078, 15713),
        (0, 23, 57, 15, 59, 50, 59, 15, 30),
        (0, 58, 110, 86, 88, 59, 94, 93, 52),
        (1, NONE, 76835, NONE, NONE, NONE, NONE, NONE, NONE),
        (0, 21, 19, 21, 18, 27, 14, 20, 65),
        (0, 65, 87, 110, 118, 103, 110, 58, 102),
        (0, 30, 99, 58, 60, 58, 22, NONE, 92),
        (0, 106, 108, 87, 93, 117, 50, NONE, 98),
        (1, 76650, 78891, NONE, NONE, NONE, NONE, 28022, 13666),
        (0, 29, 14, 27, 20, 22, 58, 59, 34),
        (0, 66, 95, 118, 95, 101, 109, 99, 53),
        (0, 27, 22, 11, 14, 13, 15, 94, 1),
        (0, 114, 27, 59, 94, 110, 99, 60, 86),
        (1, 78706, 80947, NONE, NONE, NONE, NONE, NONE, NONE),
        (0, 35, 30, 60, 22, 43, 28, 112, 42),
        (0, 67, 58, 100, 50, 52, 29, 100, 101),
        (0, 43, 45, 37, 27, 14, 19, 51, 50),
        (0, 68, 29, 95, 103, 102, 117, 90, 94),
        (0, 28, 59, 6, 52, 21, 51, 42, 23),
        (0, 136, 21, 101, 58, 51, 100, 52, 99),
        (0, 51, 44, 45, 28, 36, 21, 101, 58),
        (0, 69, 53, 103, 102, 108, 101, 43, 108),
        (0, 37, 46, 14, 53, 109, 108, 50, 110),
        (0, 86, 52, 28, 101, 20, 43, 108, 35),
        (0, 59, 28, 53, 13, 44, 44, 35, 118),
        (0, 70, 54, 94, 51, 28, 20, 44, 43),
        (0, 44, 60, 36, 36, NONE, NONE, NONE, 44),
        (0, 61, 37, 102, 109, NONE, NONE, NONE, 93),
        (0, 36, 36, 29, 21, NONE, NONE, NONE, 51),
        (0, 52, 61, 44, 44, NONE, NONE, NONE, 117),
        (0, 53, NONE, NONE, NONE, NONE, NONE, NONE, 100),
        (0, 60, NONE, NONE, NONE, NONE, NONE, NONE, 109),
    ),
    (
        (1, 16200, 14144, 14144, 86344, 86344, 86344, 86344, 32576),
        (1, 67912, 86344, 86344, 16200, 16200, 16200, 16200, 86344),
        (1, 131144, 132429, 131915, 131658, 131144, 131144, 131144, 168504),
        (1, 69968, 16200, 16200, 14144, 12088, 14144, 12088, 34632),
        (1, 12088, 86601, 86601, 86601, 86601, 86601, 86601, 86601),
        (1, 131401, 131401, 131144, 131144, 131401, 131401, 131401, 169000),
        (1, 68169, 86858, 86858, 86858, 10032, 86858, 14144, 18184),
        (1, 14144, 18256, 17999, 18256, 86858, 18256, 71952, 69896),
        (1, 68683, 69896, 87372, 10032, 87115, 10032, 10032, 26408),
        (1, 17999, 12088, 18256, 87115, 17999, 69896, 69896, 86858),
        (1, 131658, 131658, 131401, 131401, 131658, 131658, 131658, 168752),
        (1, 68940, 87115, 12088, 12088, 18256, 12088, 86858, 28464),
        (1, 18256, 17999, 69896, 87372, 69896, 71952, 17999, 87115),
        (1, 131915, 132172, 131658, 131915, 131915, 131915, 131915, 168256),
        (1, 132172, 10032, 17742, 17742, 132172, 132172, 87115, 87372),
        (1, 7976, 131144, 10032, 17999, 71952, 17485, 132172, 87629),
        (1, 132429, 71952, 132172, 132172, 132429, 74008, 87372, 131144),
        (1, 68426, 74008, 132429, 132429, 7976, 132429, 132429, 87886),
        (1, 10032, NONE, 71952, NONE, 74008, 17742, 7976, 169744),
        (1, NONE, NONE, NONE, NONE, NONE, NONE, 87629, 71952),
        (0, 81, 63, 55, 55, 63, 63, 63, 9),
        (0, 127, 81, 81, 81, 81, 81, 81, 63),
        (1, 70225, 13887, 88657, 88657, 13887, 13887, 13887, 32319),
        (1, 30335, 88657, 11831, 11831, 88657, 88657, 88657, 74008),
        (1, 17228, 16971, 74008, 69896, 14144, 87115, 87886, 30520),
        (1, 69197, 76064, 133457, 132686, 132686, 17999, 22792, 169496),
        (1, 132686, NONE, NONE, NONE, NONE, 132686, 132686, NONE),
        (0, 82, 47, 63, 63, 55, 47, 55, 17),
        (0, 135, 82, 82, 82, 82, 82, 82, 47),
        (1, 70482, 88914, 88914, 88914, 11831, 9775, 11831, 28207),
        (1, 32391, 9775, 13887, 13887, 88914, 88914, 88914, 70153),
        (1, NONE, 131915, 87629, NONE, 132943, 132943, 132943, 169248),
        (0, 71, 55, 71, 70, 71, 25, 17, 10),
        (0, 83, 83, 83, 83, 83, 39, 71, 55),
        (1, 70739, 133971, 89171, 89171, 15943, 74265, 15943, 30263),
        (1, 17485, 11831, 15943, 15686, 89171, 7719, 74008, 72209),
        (1, NONE, NONE, NONE, 17485, 17228, 87372, NONE, NONE),
        (1, NONE, NONE, NONE, 71952, NONE, NONE, NONE, NONE),
        (0, 17, 70, 47, 71, 17, 17, 39, 12),
        (0, 103, 85, 84, 84, 39, 70, 83, 39),
        (1, 133457, 134485, 9775, 89428, 17485, 15686, 72209, 26151),
        (1, NONE, 17485, 89428, 15943, 76064, 87629, 133457, 131658),
        (1, NONE, 78120, 17485, 74008, 133457, 133457, NONE, NONE),
        (1, NONE, NONE, 133714, 7976, NONE, NONE, NONE, NONE),
        (1, NONE, NONE, NONE, 132943, NONE, NONE, NONE, NONE),
        (0, 84, 17, 70, 17, 25, 71, 47, 13),
        (0, 111, 71, 85, 47, 47, 83, 84, 70),
        (1, 17742, 17742, 87115, 9775, 17742, 15943, 9775, 76064),
        (1, 134228, 72209, 5920, 76064, 72209, 72209, 76064, 131915),
        (1, NONE, 132686, 134228, 133457, 133714, 133714, 133714, NONE),
        (0, 145, 136, 128, 104, 136, 112, 104, 88),
        (1, 86673, NONE, NONE, NONE, 32648, NONE, 24424, NONE),
        (0, 90, 90, 54, 69, 69, 54, 54, 18),
        (0, 126, 118, 90, 90, 90, 90, 85, 54),
        (1, 30078, 90970, 135770, 90970, 90970, 11574, 11574, 30006),
        (1, 72538, 28022, 11574, 15429, 74265, 90970, 78120, 72466),
        (1, 70996, 5920, 76064, 72209, 5920, 76064, 16971, 78120),
        (1, 3864, NONE, 7976, NONE, NONE, 26480, NONE, NONE),
        (0, 91, 91, 39, 39, 70, 46, 38, 19),
        (0, 110, 126, 91, 91, 91, 84, 86, 46),
        (2,),
        (1, 140910, 91227, 91227, 136027, 91227, 225320, 7462, 27950),
        (1, 233801, 30078, 229432, 223264, 231488, NONE, 223264, 219152),
        (1, NONE, 231488, NONE, NONE, NONE, NONE, NONE, NONE),
        (0, 0, 5, 3, 2, 0, 0, 0, 146),
        (1, 72795, 133457, 15686, 7719, 7719, 78120, 17228, 12178),
        (1, 5920, NONE, 78120, 133714, 133971, 9518, 89171, 70410),
        (1, NONE, NONE, 134485, NONE, NONE, 133971, 133971, 132172),
        (0, 146, 144, 136, 120, 127, 136, 96, 96),
        (1, 86930, NONE, NONE, NONE, NONE, NONE, NONE, NONE),
        (0, 25, 31, 38, 25, 33, 62, 68, 20),
        (0, 118, 92, 92, 46, 46, 85, 87, 62),
        (1, 28022, 136284, 7719, 74265, 9775, 32648, 17485, 70924),
        (1, 15943, 87372, 68611, 9518, 76321, 89171, 221208, 221208),
        (1, 234058, 7976, 231488, 227376, 229175, 231488, NONE, NONE),
        (1, NONE, 233544, NONE, NONE, NONE, NONE, NONE, NONE),
        (0, 1, 1, 0, 0, 1, 1, 1, 148),
        (1, 135770, 133714, 136027, 133971, 135770, 135770, 134228, 8084),
        (1, NONE, NONE, NONE, NONE, NONE, NONE, NONE, 132429),
        (0, 88, 88, 119, 128, 112, 135, 120, 104),
        (1, 72024, NONE, NONE, NONE, NONE, NONE, NONE, NONE),
        (0, 33, 25, 46, 33, 34, 31, 25, 11),
        (0, 102, 39, 93, 54, 54, 86, 69, 31),
        (1, NONE, 74265, 7462, 76321, 15429, 13630, 74265, 71181),
        (1, NONE, 15686, NONE, 78120, 76578, NONE, 17742, NONE),
        (1, NONE, 68097, NONE, NONE, NONE, NONE, NONE, NONE),
        (0, 41, 33, 17, 62, 61, 55, 33, 14),
        (0, 119, 67, 66, 92, 84, 87, 70, 89),
        (1, 219152, 76321, 72209, 13630, 225320, 231231, 76321, 15961),
        (1, NONE, 219152, 227119, 229432, NONE, NONE, 227376, 223264),
        (0, 2, 2, 1, 1, 2, 2, 2, 147),
        (1, 16714, 15943, 9518, 134228, 15686, 32391, 18256, 10131),
        (1, 145022, 135770, 136284, NONE, 87372, 134228, 134485, 72723),
        (1, NONE, NONE, NONE, NONE, 136027, NONE, NONE, 132686),
        (0, 144, 96, 144, 136, 120, 104, 128, 112),
        (1, 86416, NONE, NONE, NONE, NONE, NONE, NONE, NONE),
        (0, 99, 86, 99, 38, 62, 91, 18, 45),
        (0, 117, 117, 109, 99, 99, 127, 45, 82),
        (1, 142709, 27765, 16971, 7462, 93283, 80176, 72466, 27693),
        (1, 16971, 5663, 233544, 16971, 11574, 30335, 22368, 72980),
        (1, 233544, 80176, NONE, 231488, 227376, 223264, 229432, 22296),
        (1, NONE, 221208, NONE, NONE, NONE, NONE, NONE, 225320),
        (0, 3, 4, 2, 3, 3, 3, 3, 145),
        (1, 136027, 136027, 136541, 135770, 134228, 134485, 134742, 14225),
        (1, NONE, NONE, NONE, NONE, NONE, NONE, NONE, 132943),
        (0, 96, 104, 88, 144, 128, 120, 135, 90),
        (1, 74080, NONE, NONE, NONE, NONE, NONE, NONE, NONE),
        (0, 100, 68, 25, 45, 68, 33, 26, 27),
        (0, 109, 93, 117, 100, 85, 67, 30, 95),
        (1, 69454, 7719, 74265, 17228, 78120, 76321, 74522, 88914),
        (1, 1808, 68354, 17228, NONE, 13373, 5920, 15172, 24352),
        (1, NONE, NONE, NONE, NONE, NONE, 82232, NONE, NONE),
        (0, 47, 100, 33, 41, 31, 26, 27, 38),
        (1, 9775, NONE, NONE, NONE, NONE, NONE, NONE, NONE),
        (0, 49, 109, 68, 68, 86, 68, 61, 83),
        (1, 221208, 223264, 76321, 78377, 229432, 74522, 74779, 219666),
        (1, NONE, NONE, 219152, 233544, NONE, 227376, 231231, NONE),
        (0, 4, 0, 4, 4, 4, 4, 4, 0),
        (1, 74851, 16714, 3864, 3864, 82232, 7976, 28536, 16128),
        (1, 24167, 68868, 138083, 136284, 13630, 87886, 80176, 74779),
        (1, 142966, 134742, NONE, NONE, 138083, 134742, 134999, 24095),
        (1, NONE, NONE, NONE, NONE, NONE, NONE, NONE, 155974),
        (0, 104, 112, 96, 96, 118, 128, 111, 120),
        (1, 76136, NONE, NONE, NONE, NONE, NONE, NONE, NONE),
        (0, 31, 69, 41, 23, 26, 41, 41, 25),
        (0, 26, 84, 69, 26, 38, 69, 62, 29),
        (1, 75108, 89428, 78377, 74522, 74522, 16971, 82232, 89171),
        (1, 26223, 17228, 28279, 5920, 16971, 89428, 15429, 25894),
        (1, 223264, 69125, 221208, 221208, 87629, 229432, 225063, 227376),
        (1, NONE, 225320, NONE, NONE, 226862, NONE, NONE, NONE),
        (0, 5, 11, 5, 5, 5, 5, 5, 151),
        (0, 39, NONE, NONE, NONE, NONE, NONE, NONE, NONE),
        (1, 138854, 142709, 140653, 138083, 134485, 134999, NONE, 156222),
        (0, 89, 120, 104, 126, 144, 144, 110, 103),
        (1, 72281, NONE, NONE, NONE, NONE, NONE, NONE, NONE),
        (0, 34, 15, 23, 31, 41, 23, 49, 21),
        (0, NONE, 41, 26, 34, 60, 49, 103, 66),
        (1, 25966, 1808, 74522, 76578, 30335, 17228, 15686, 74265),
        (1, NONE, 70667, 14658, 80176, 87886, 89685, 88143, 1943),
        (0, 42, 23, NONE, NONE, 30, 30, 19, 28),
        (0, 108, 49, NONE, NONE, 49, 92, 37, 67),
        (1, 219409, 227376, NONE, 24424, 233544, 233544, 224806, 223007),
        (0, 6, 13, 34, 61, 6, 6, 6, 150),
        (1, 28279, 3864, NONE, NONE, 9518, 11831, 30592, 23581),
        (1, 138083, 136541, NONE, NONE, 88143, 91227, 89428, 80176),
        (0, 112, 128, 108, 108, NONE, NONE, NONE, NONE),
        (1, 78192, NONE, 76578, 228918, 134742, 136027, NONE, 131401),
        (0, 62, 12, NONE, NONE, 88, 96, 117, 128),
        (1, NONE, 70924, 223264, NONE, NONE, NONE, NONE, NONE),
        (0, 85, 62, 9, 6, 37, 34, 21, 68),
        (0, NONE, NONE, NONE, NONE, 92, 38, 127, 81),
        (1, 71253, 14915, 15172, 11574, 15172, 24424, 32391, 82232),
        (1, 27765, 78377, 80176, 87629, 89428, 78377, 89685, 3990),
        (1, 225320, 229432, 142709, 138340, 219152, 221208, 226605, 229432),
        (0, 38, 3, 112, 112, 7, 7, 7, 149),
        (0, 10, 38, 31, 30, NONE, NONE, NONE, NONE),
        (0, 55, NONE, 42, 42, NONE, NONE, NONE, NONE),
        (1, 138340, 138340, 78634, 78634, NONE, NONE, NONE, 137055),
        (0, 120, 135, NONE, NONE, 96, 119, 136, 136),
        (0, NONE, 26, NONE, NONE, 42, 42, 22, 33),
        (0, NONE, NONE, NONE, NONE, 53, 60, 53, 69),
        (1, 80248, 15172, 15429, 15172, 89685, 80433, 78377, 70667),
        (1, 5663, 80433, 90970, 87886, 5663, 14915, 13373, 6037),
        (0, 63, 34, NONE, NONE, 29, 27, 28, 41),
        (0, 93, 65, NONE, NONE, 35, 61, 126, 71),
        (1, 73309, 231231, 225320, 225320, 221208, 227119, 231488, 231488),
        (0, NONE, NONE, NONE, NONE, 9, 9, 9, 2),
        (1, 227376, NONE, NONE, NONE, 78377, 15172, 26223, 90970),
        (1, NONE, NONE, NONE, NONE, 28022, 91484, 80433, 16642),
        (0, 9, 20, 18, 19, 104, 111, 144, 144),
        (0, NONE, NONE, NONE, NONE, 57, 35, 29, 26),
        (0, NONE, NONE, NONE, NONE, 66, 45, 118, 87),
        (1, 7462, 15429, 140396, 140396, 7462, 76578, 72723, 94311),
        (1, 140653, 71181, NONE, NONE, 80433, 15429, 13630, 233544),
        (1, NONE, 140653, NONE, NONE, 223264, 225063, 233544, NONE),
        (0, 128, 119, 120, 117, 10, 10, 10, 3),
        (1, 82304, NONE, NONE, NONE, NONE, NONE, NONE, 16899),
        (0, 57, 42, 49, 29, 135, 126, 88, 135),
        (0, 87, 66, 61, 43, 65, 36, 23, 15),
        (1, 7719, 1551, 3607, 78891, NONE, NONE, NONE, NONE),
        (0, NONE, NONE, NONE, NONE, 67, 52, 91, 59),
        (1, 229432, 72980, 72466, 30078, 13116, 78634, 91227, 88657),
        (1, NONE, 227119, NONE, 68354, 91484, 13116, 25966, NONE),
        (0, 12, 6, 50, 37, 15, 53, 31, 36),
        (0, 11, 127, 62, 85, 87, 57, 36, 111),
        (1, 140396, NONE, 227376, 226605, 231231, 228918, 219152, 231231),
        (0, 97, 7, 10, 7, 11, 11, 11, 4),
        (1, 74337, NONE, 5663, 91227, 78634, 74779, 24167, 17156),
        (1, NONE, NONE, 80433, 5663, 5406, 13373, NONE, 76321),
        (0, 95, 50, 127, 127, 111, 103, 119, 127),
        (1, 13630, 3607, NONE, NONE, NONE, NONE, NONE, NONE),
        (0, 13, NONE, 22, 35, 23, 65, 66, 37),
        (0, 94, NONE, 35, 66, 93, 66, 92, 60),
        (1, 221465, 74522, 13373, 91484, 11317, 76835, 91484, 78377),
        (1, NONE, NONE, 80690, 13373, 76835, 11060, 27765, 229175),
        (1, NONE, NONE, 229175, 229175, 225063, 223007, NONE, NONE),
        (0, 45, 35, 12, 9, 18, 18, NONE, 5),
        (1, 9261, NONE, NONE, NONE, NONE, NONE, 227119, 17413),
        (0, 105, 94, 135, 135, 119, 95, 12, 84),
        (1, 76393, 229175, NONE, NONE, NONE, NONE, NONE, NONE),
        (0, 14, 9, 30, 49, 94, 88, 102, 49),
        (0, 101, NONE, 43, 67, 95, 118, 34, 61),
        (1, 11831, 76578, 13630, 5406, 5149, 11317, NONE, 74522),
        (1, 223521, 13630, 76835, 72723, NONE, NONE, NONE, NONE),
        (0, 18, 103, 51, 15, 45, 37, 67, 22),
        (0, 7, 43, 65, 65, 100, 93, NONE, 119),
        (0, 20, 102, NONE, NONE, NONE, NONE, NONE, NONE),
        (1, NONE, 78634, 231231, 231231, 227119, 220951, 76578, 218124),
        (0, 113, NONE, 13, 10, 19, 12, NONE, 6),
        (1, 78449, 7462, 3350, 27765, NONE, NONE, 30335, 17670),
        (1, 13887, 223007, 78891, 89685, NONE, NONE, NONE, NONE),
        (0, 21, 10, 126, 119, 126, 102, 46, 85),
        (0, 92, 111, 52, 86, 50, 59, 57, 57),
        (0, NONE, NONE, 67, 110, 59, 94, NONE, 126),
        (1, 225577, NONE, 5406, 5149, 228918, 222750, 222750, 218381),
        (1, NONE, NONE, 80947, 76835, NONE, NONE, NONE, NONE),
        (0, 54, 51, NONE, NONE, 12, 13, 13, 7),
        (0, 121, 101, NONE, NONE, NONE, NONE, NONE, NONE),
        (1, 80505, 80690, 228918, 227119, NONE, NONE, 11317, 17927),
        (0, 15, 57, 19, 11, 103, 110, 109, 91),
        (0, 50, 110, 111, 111, 58, 22, 65, 30),
        (1, 227633, 225063, NONE, NONE, NONE, NONE, NONE, NONE),
        (0, 19, 18, 7, 57, 117, 50, 95, 52),
        (0, 23, NONE, 57, 87, 22, 58, NONE, 65),
        (0, 98, NONE, NONE, NONE, 101, 109, NONE, 102),
        (1, 74594, 76835, 81204, 7205, 223007, 224806, 30078, 219923),
        (0, 58, 87, 15, 59, 27, 14, NONE, 97),
        (0, 22, 99, 86, 88, NONE, NONE, NONE, NONE),
        (0, 65, 108, NONE, NONE, NONE, NONE, NONE, NONE),
        (1, 221722, 78891, 225063, 225063, NONE, NONE, 224549, 15713),
        (0, 46, NONE, 20, 12, 110, 99, 14, 92),
        (0, 106, NONE, 110, 118, 43, 28, 93, 34),
        (1, 76650, 218895, NONE, NONE, NONE, NONE, NONE, NONE),
        (0, 29, 19, 58, 60, 52, 29, 20, 53),
        (0, 66, 22, 87, 93, NONE, NONE, NONE, NONE),
        (1, 223778, NONE, 224806, 226862, 224806, 221979, NONE, 220180),
        (0, 30, 27, 21, 18, 13, 15, 58, 98),
        (1, NONE, NONE, NONE, NONE, NONE, NONE, 28022, 13666),
        (0, 67, 95, 11, 95, 102, 117, 59, 86),
        (0, 114, NONE, 118, 14, 21, 51, 99, 42),
        (1, 78706, 80947, NONE, NONE, NONE, NONE, NONE, NONE),
        (0, 35, 29, 59, 94, 51, 100, NONE, 101),
        (0, 68, 58, 60, 22, 36, 21, NONE, 50),
        (0, 43, NONE, 100, 50, 108, 101, NONE, 94),
        (1, 225834, 220951, 226862, 220951, 222750, 226605, 220437, 218638),
        (0, 27, 14, 27, 20, 14, 19, 15, 1),
        (0, 136, 30, 95, 103, 109, 108, 94, 99),
        (0, 69, 59, 6, 52, 20, 43, 60, 58),
        (0, 51, 45, 101, 58, 44, 44, 112, 108),
        (1, 231488, NONE, 220951, 223007, 224549, 224292, 220694, 221979),
        (0, 28, 44, 37, 27, 28, 20, 100, 23),
        (0, 61, 53, 28, 102, NONE, NONE, 51, 110),
        (0, 86, 36, 103, 53, NONE, NONE, 90, 35),
        (0, 59, 52, 14, 101, NONE, NONE, 42, 118),
        (0, 53, 21, 53, 13, NONE, NONE, 52, 43),
        (0, 44, 46, 94, 51, NONE, NONE, NONE, 44),
        (1, 218638, NONE, 223007, 222750, NONE, NONE, 222236, 224806),
        (0, 37, 60, 45, 28, NONE, NONE, 101, 93),
        (0, 70, 28, 102, 109, NONE, NONE, 43, 51),
        (0, 52, 54, 29, 21, NONE, NONE, 50, 117),
        (0, 36, 61, 44, 44, NONE, NONE, NONE, NONE),
        (1, NONE, NONE, 222750, 224549, NONE, NONE, 222493, 220437),
        (0, 60, 37, 36, 36, NONE, NONE, 108, 100),
        (0, NONE, NONE, NONE, NONE, NONE, NONE, 35, 109),
        (0, NONE, NONE, NONE, NONE, NONE, NONE, 44, NONE),
        (1, NONE, NONE, NONE, NONE, NONE, NONE, 224292, 222236),
    ),
)
OWN = BAND * HALF


def device_of(row, cols):
    return row // cols, lax.rem(row, cols)


def kernel(cols_hbm, blocks_hbm, out_ref, cols_ref, blocks_ref, own, square, upper, flipped, newband, in_sem, entered, send_sem, recv_sem):
    size = blocks_ref.shape[-1]
    loads = [
        pltpu.make_async_copy(cols_hbm, cols_ref, in_sem.at[0]),
        pltpu.make_async_copy(blocks_hbm, blocks_ref, in_sem.at[1]),
    ]
    for load in loads:
        load.start()
    cols = lax.axis_size("col")
    count = cols * lax.axis_size("row")
    me = lax.axis_index("row") * cols + lax.axis_index("col")
    place = lax.rem(me, RING)
    start = me - place
    targets = (
        start + lax.rem(place + 1, RING),
        start + lax.rem(place + RING - 1, RING),
        lax.rem(me + RING, count),
        lax.rem(me + count - RING, count),
    )
    barrier = pltpu.get_barrier_semaphore()
    peers = [device_of(target, cols) for target in targets]
    for peer in (peers[0], peers[1], peers[3]):
        pl.semaphore_signal(barrier, inc=1, device_id=peer, device_id_type=MESH)

    bits = [lax.rem(place // 2**n, 2) == 1 for n in range(3)]

    def pick(values):
        for bit in bits:
            values = [jnp.where(bit, high, low) for low, high in zip(values[::2], values[1::2])]
        return values[0]

    for load in loads:
        load.wait()
    missing = jnp.int32(0)
    for s in range(WINDOW - 1):
        offset = lax.rem(cols_ref[0, s] - me + BAND + count, count)
        missing += jnp.where(offset == s, 1, 0)

    for o in range(WINDOW):
        first = blocks_ref[0, min(o, WINDOW - 2)]
        second = blocks_ref[0, max(o - 1, 0)]
        block = jnp.where(o < missing, first, jnp.where(o == missing, jnp.zeros_like(first), second))
        own[:, o * size : (o + 1) * size] = block
        if o >= BAND:
            upper[OWN + o - BAND] = block
        else:
            slot = o * HALF + BAND - o
            upper[slot] = block.T
            flipped[slot] = block

    for d in range(HALF):
        flipped[OWN + d] = upper[OWN + d].T
    pl.semaphore_wait(barrier, 3)
    pl.semaphore_signal(entered, inc=1, device_id=peers[2], device_id_type=MESH)

    def copy(here, there, peer):
        return pltpu.make_async_remote_copy(
            src_ref=upper.at[here],
            dst_ref=upper.at[there],
            send_sem=send_sem,
            recv_sem=recv_sem.at[there],
            device_id=peer,
            device_id_type=MESH,
        )

    def send(code):
        direction = code >> 16
        ahead, far = (direction & 1) == 0, direction >= 2
        peer = tuple(
            jnp.where(far, jnp.where(ahead, c, d), jnp.where(ahead, a, b)) for a, b, c, d in zip(*peers)
        )
        copy(code & 255, (code >> 8) & 255, peer).start()

    def receive(here):
        copy(here, here, peers[0]).wait_recv()

    def turn(here):
        flipped[here] = upper[here].T

    def where_any(codes, code, action):
        if NONE in codes:
            pl.when(code != NONE)(functools.partial(action, code))
        else:
            action(code)

    def exchange(events):
        unturned, sending = [], False
        for kind, *codes in events:
            code = pick([jnp.int32(c) for c in codes]) if codes else None
            if kind == 1:
                where_any(codes, code, send)
            elif kind == 2:
                pl.semaphore_wait(entered, 1)
            else:
                if sending:
                    for late in unturned:
                        where_any(*late, turn)
                    unturned = []
                where_any(codes, code, receive)
                unturned.append((codes, code))
            sending = kind == 1
        for late in unturned:
            where_any(*late, turn)

    ring = lax.rem(me // RING, 16)
    ring = jnp.where((ring == 0) | (ring == 4), 1, 0)
    sends = jnp.int32(0)
    for n, events in enumerate(EVENTS):
        pl.when(ring == n)(functools.partial(exchange, events))
        counts = [sum(e[0] == 1 and e[1 + y] != NONE for e in events) for y in range(RING)]
        sends = jnp.where(ring == n, pick([jnp.int32(c) for c in counts]), sends)
    def block_at(k, j):
        if abs(k - j) > BAND:
            return jnp.zeros((size, size), upper.dtype)
        return upper[k * HALF + j - k] if k <= j else flipped[j * HALF + k - j]

    def product(factor, first, width):
        low, high = max(0, first - BAND), min(WINDOW, first + width + BAND)
        columns = [
            jnp.concatenate([block_at(k, j) for k in range(low, high)], axis=0) for j in range(first, first + width)
        ]
        return jnp.dot(
            factor[:, low * size : high * size],
            jnp.concatenate(columns, axis=1),
            preferred_element_type=jnp.float32,
        )

    for first in range(0, WINDOW, 2):
        width = min(2, WINDOW - first)
        total = product(own, first, width)
        for w in range(width):
            piece = total[:, w * size : (w + 1) * size]
            piece = jnp.where(missing == first + w, 0.0, piece).astype(square.dtype)
            square[:, (first + w) * size : (first + w + 1) * size] = piece
    for first in range(0, WINDOW, 2):
        width = min(2, WINDOW - first)
        total = product(square, first, width)
        for w in range(width):
            part = slice((first + w) * size, (first + w + 1) * size)
            value = 3.0 * square[:, part].astype(jnp.float32) - 2.0 * total[:, w * size : (w + 1) * size]
            newband[first + w] = value.astype(newband.dtype)
    for s in range(WINDOW - 1):
        out_ref[0, s] = jnp.where(s < missing, newband[s], newband[s + 1])

    for number in sorted({sum(e[0] == 1 and e[1 + y] != NONE for e in events) for events in EVENTS for y in range(RING)}):
        blocks = upper.at[pl.ds(0, number)]
        pl.when(sends == number)(lambda blocks=blocks: pltpu.make_async_copy(blocks, blocks, send_sem).wait())


def per_device(block_cols, blocks):
    size = blocks.shape[-1]
    kind = blocks.dtype
    return pl.pallas_call(
        kernel,
        out_shape=jax.ShapeDtypeStruct(blocks.shape, kind),
        in_specs=[pl.BlockSpec(memory_space=pltpu.HBM)] * 2,
        out_specs=pl.BlockSpec(memory_space=pltpu.VMEM),
        scratch_shapes=[
            pltpu.SMEM(block_cols.shape, block_cols.dtype),
            pltpu.VMEM(blocks.shape, kind),
            pltpu.VMEM((size, WINDOW * size), kind),
            pltpu.VMEM((size, WINDOW * size), kind),
            pltpu.VMEM((WINDOW * HALF, size, size), kind),
            pltpu.VMEM((WINDOW * HALF, size, size), kind),
            pltpu.VMEM((WINDOW, size, size), kind),
            pltpu.SemaphoreType.DMA((2,)),
            pltpu.SemaphoreType.REGULAR,
            pltpu.SemaphoreType.DMA,
            pltpu.SemaphoreType.DMA((WINDOW * HALF,)),
        ],
        compiler_params=pltpu.CompilerParams(collective_id=0, has_side_effects=True, vmem_limit_bytes=40 * 2**20),
        cost_estimate=pl.CostEstimate(flops=4 * 217 * size**3, bytes_accessed=2 * 2**20, transcendentals=0),
        name="purify",
    )(*(pltpu.with_memory_space_constraint(x, pltpu.HBM) for x in (block_cols, blocks)))


def solution(mesh):
    placed = (P(("row", "col"), None), P(("row", "col"), None, None, None))
    return jax.shard_map(
        per_device,
        mesh=mesh,
        in_specs=placed,
        out_specs=P(("row", "col"), None, None, None),
        check_vma=False,
    )
```

```python
import functools

import jax
import jax.numpy as jnp
from jax import lax
from jax.experimental import pallas as pl
from jax.experimental.pallas import tpu as pltpu
from jax.sharding import PartitionSpec as P

BAND = 8
WINDOW = 2 * BAND + 1
HALF = BAND + 1
RING = 8
MESH = pl.DeviceIdType.MESH

NONE = 2**18
EVENTS = (
    (
        (1, 16200, 14144, 14144, 86344, 86344, 86344, 86344, 168504),
        (1, 67912, 86344, 86344, 16200, 16200, 16200, 16200, 32576),
        (1, 131144, 132429, 131915, 131658, 131144, 131144, 131144, 86344),
        (1, 69968, 16200, 16200, 14144, 12088, 14144, 12088, 34632),
        (1, 12088, 86601, 86601, 86601, 86601, 86601, 86601, 86601),
        (1, 131401, 131401, 131144, 131144, 131401, 131401, 131401, 169000),
        (1, 68169, 86858, 86858, 86858, 10032, 86858, 14144, 18184),
        (1, 14144, 18256, 17999, 18256, 86858, 18256, 71952, 69896),
        (1, 131658, 131658, 131401, 10032, 131658, 10032, 10032, 26408),
        (1, 68683, 69896, 87372, 131401, 87115, 131658, 131658, 168752),
        (1, 17999, 12088, 18256, 87115, 17999, 69896, 69896, 86858),
        (1, 68940, 87115, 12088, 12088, 18256, 12088, 86858, 28464),
        (1, 18256, 17999, 69896, 87372, 69896, 71952, 17999, 87115),
        (2,),
        (1, 233801, 231488, 229432, 223264, 231488, 225320, 223264, 219152),
        (1, 131915, 132172, 131658, 131915, 131915, 131915, 131915, 168256),
        (1, 234058, 233544, 17742, 17742, 132172, 231488, 221208, 87372),
        (1, 132172, 131144, 231488, 227376, 71952, 132172, 87115, 221208),
        (1, 7976, 10032, 132172, 132172, 225320, 17485, 132172, 131144),
        (1, 219152, 71952, 10032, 17999, 132429, 74008, 87372, 87629),
        (1, 132429, 219152, 132429, 229432, 7976, 132429, 227376, 87886),
        (1, 68426, 74008, 71952, 132429, 74008, 17742, 132429, 223264),
        (1, 10032, NONE, NONE, NONE, NONE, NONE, 7976, 169744),
        (1, NONE, NONE, NONE, NONE, NONE, NONE, 87629, 71952),
        (0, 81, 63, 55, 55, 63, 63, 63, 9),
        (0, 127, 81, 81, 81, 81, 81, 81, 63),
        (1, 70225, 13887, 88657, 88657, 13887, 13887, 13887, 32319),
        (1, 30335, 88657, 11831, 11831, 88657, 88657, 88657, 225320),
        (1, 233544, 221208, 233544, 231488, 227376, 231231, 229432, 74008),
        (1, 17228, 16971, 133457, 132686, 14144, 223264, 87886, 169496),
        (1, 69197, 76064, 74008, 69896, 132686, 87115, 132686, 30520),
        (1, 132686, NONE, NONE, NONE, NONE, 132686, 22792, NONE),
        (1, NONE, NONE, NONE, NONE, NONE, 17999, NONE, NONE),
        (0, 82, 47, 63, 63, 55, 47, 55, 17),
        (0, 135, 82, 82, 82, 82, 82, 82, 47),
        (1, 70482, 88914, 88914, 88914, 229175, 9775, 11831, 28207),
        (1, 32391, 9775, 13887, 13887, 11831, 88914, 88914, 70153),
        (1, 221208, 223264, 87629, 233544, 88914, 227376, 231231, 169248),
        (1, NONE, 131915, 219152, NONE, 229432, 132943, 132943, NONE),
        (1, NONE, NONE, NONE, NONE, 132943, NONE, NONE, NONE),
        (0, 71, 55, 71, 70, 71, 25, 17, 10),
        (0, 83, 83, 83, 83, 83, 39, 71, 55),
        (1, 70739, 133971, 89171, 89171, 15943, 74265, 15943, 30263),
        (1, 17485, 11831, 15943, 15686, 89171, 7719, 74008, 72209),
        (1, NONE, NONE, NONE, 17485, 17228, 87372, NONE, NONE),
        (1, NONE, NONE, NONE, 71952, NONE, NONE, NONE, NONE),
        (0, 17, 70, 47, 71, 17, 17, 39, 12),
        (0, 103, 85, 84, 84, 39, 70, 83, 39),
        (1, 223264, 134485, 227119, 89428, 133457, 229432, 225063, 26151),
        (1, 133457, 225320, 9775, 15943, 17485, 133457, 133457, 227376),
        (1, NONE, 17485, 89428, 221208, 76064, 15686, 72209, 131658),
        (1, NONE, 78120, 221208, 132943, NONE, 87629, NONE, NONE),
        (1, NONE, NONE, 17485, 74008, NONE, NONE, NONE, NONE),
        (1, NONE, NONE, 133714, 7976, NONE, NONE, NONE, NONE),
        (0, 84, 17, 70, 17, 25, 71, 47, 13),
        (0, 111, 71, 85, 47, 47, 83, 84, 70),
        (1, 17742, 17742, 87115, 9775, 17742, 15943, 9775, 76064),
        (1, 219409, 72209, 5920, 76064, 72209, 72209, 76064, 131915),
        (1, 134228, 227376, 223264, 133457, 233544, 233544, 133714, NONE),
        (1, NONE, 132686, 134228, NONE, 133714, 133714, NONE, NONE),
        (0, 0, 5, 3, 2, 0, 0, 0, 88),
        (0, 145, 136, 128, 104, 136, 112, 104, 146),
        (1, 86673, NONE, NONE, NONE, 32648, NONE, 24424, 12178),
        (0, 90, 90, 54, 69, 69, 54, 54, 18),
        (0, 126, 118, 90, 90, 90, 90, 85, 54),
        (1, 30078, 90970, 135770, 90970, 90970, 11574, 11574, 30006),
        (1, 72538, 28022, 11574, 15429, 74265, 90970, 78120, 219666),
        (1, 70996, 5920, 76064, 72209, 5920, 76064, 16971, 72466),
        (1, 3864, NONE, 7976, NONE, NONE, 26480, NONE, 78120),
        (0, 91, 91, 39, 39, 70, 46, 38, 19),
        (0, 110, 126, 91, 91, 91, 84, 86, 46),
        (1, 140910, 91227, 91227, 136027, 91227, 221208, 7462, 27950),
        (1, 225320, 30078, 225320, 225320, 219152, 78120, 224806, 229432),
        (1, 72795, 229432, 134485, 133714, 7719, 9518, 17228, 70410),
        (1, 5920, 133457, 15686, 7719, 133971, 133971, 89171, 132172),
        (1, NONE, NONE, 78120, NONE, NONE, NONE, 133971, NONE),
        (0, 1, 1, 0, 0, 1, 1, 1, 96),
        (0, 146, 144, 136, 120, 127, 136, 96, 148),
        (1, 86930, NONE, NONE, NONE, NONE, NONE, NONE, 8084),
        (0, 25, 31, 38, 25, 33, 62, 68, 20),
        (0, 118, 92, 92, 46, 46, 85, 87, 62),
        (1, 28022, 136284, 68611, 74265, 226862, 32648, 17485, 70924),
        (1, 15943, 87372, 7719, 9518, 9775, 89171, 231488, 231488),
        (1, 227376, 7976, 227376, 133971, 76321, 227119, 134228, 132429),
        (1, 135770, 231231, 136027, NONE, 221208, 135770, NONE, NONE),
        (1, NONE, 133714, NONE, NONE, 135770, NONE, NONE, NONE),
        (0, 2, 2, 1, 1, 2, 2, 2, 104),
        (0, 88, 88, 119, 128, 112, 135, 120, 147),
        (1, 72024, NONE, NONE, NONE, NONE, NONE, NONE, 10131),
        (0, 33, 25, 46, 33, 34, 31, 25, 11),
        (0, 102, 39, 93, 54, 54, 86, 69, 31),
        (1, NONE, 74265, 7462, 228918, 15429, 13630, 74265, 223007),
        (1, NONE, 15686, NONE, 76321, 76578, NONE, 17742, 71181),
        (1, NONE, 69125, NONE, 78120, NONE, NONE, NONE, NONE),
        (0, 41, 33, 17, 62, 61, 55, 33, 14),
        (0, 119, 67, 66, 92, 84, 87, 70, 89),
        (1, 229432, 76321, 72209, 13630, 223264, 225063, 76321, 15961),
        (1, 16714, 227119, 229175, 229175, 136027, 32391, 233544, 233544),
        (1, 145022, 135770, 136284, 134228, 15686, 134228, 18256, 72723),
        (1, NONE, 15943, 9518, NONE, 87372, NONE, 134485, 132686),
        (0, 3, 4, 2, 3, 3, 3, 3, 112),
        (0, 144, 96, 144, 136, 120, 104, 128, 145),
        (1, 86416, NONE, NONE, NONE, NONE, NONE, NONE, 14225),
        (0, 99, 86, 99, 38, 62, 91, 18, 45),
        (0, 117, 117, 109, 99, 99, 127, 45, 82),
        (1, 142709, 27765, 16971, 7462, 93283, 80176, 226605, 27693),
        (1, 16971, 5663, 231231, 16971, 11574, 30335, 72466, 72980),
        (1, 221465, 80176, 136541, 231231, 231231, 228918, 22368, 22296),
        (1, 136027, 229175, NONE, 135770, 134228, 134485, 219152, 231231),
        (1, NONE, 136027, NONE, NONE, NONE, NONE, 134742, 132943),
        (0, 4, 0, 4, 4, 4, 4, 4, 0),
        (0, 96, 104, 88, 144, 128, 120, 135, 90),
        (1, 74080, NONE, NONE, NONE, NONE, NONE, NONE, 16128),
        (0, 100, 68, 25, 45, 68, 33, 26, 27),
        (0, 109, 93, 117, 100, 85, 67, 30, 95),
        (1, 69454, 68097, 74265, 226605, 78120, 76321, 74522, 88914),
        (1, 1808, 7719, 17228, 17228, 13373, 5920, 15172, 24352),
        (1, NONE, NONE, NONE, NONE, NONE, 82232, NONE, NONE),
        (0, 47, 100, 33, 41, 31, 26, 27, 38),
        (0, 49, 109, 68, 68, 86, 68, 61, 83),
        (1, 9775, 223007, 76321, 78377, 225063, 74522, 74779, 229175),
        (1, 223521, 16714, 228918, 227119, 82232, 223007, 227119, 74779),
        (1, 74851, 68354, 138083, 136284, 138083, 7976, 28536, 24095),
        (1, 24167, 134742, 3864, 3864, 13630, 87886, 80176, 155974),
        (1, 142966, NONE, NONE, NONE, NONE, 134742, 134999, NONE),
        (0, 5, 11, 5, 5, 5, 5, 5, 120),
        (0, 104, 112, 96, 96, 118, 128, 111, 151),
        (1, 76136, NONE, NONE, NONE, NONE, NONE, NONE, NONE),
        (0, 26, 69, 41, 23, 26, 41, 41, 25),
        (0, 31, 84, 69, 26, 38, 69, 62, 29),
        (1, 75108, 89428, 78377, 74522, 74522, 16971, 82232, 89171),
        (1, 26223, 17228, 28279, 5920, 16971, 89428, 15429, 25894),
        (1, 225577, 68868, 225063, 225063, 87629, 134999, 222750, 218124),
        (1, 138854, 225063, 140653, 138083, 227119, NONE, NONE, 156222),
        (1, NONE, NONE, NONE, NONE, 134485, NONE, NONE, NONE),
        (0, 6, NONE, 9, 6, 6, 6, 6, 103),
        (0, 89, NONE, 104, 126, 144, 144, 110, 150),
        (1, 72281, 142709, NONE, NONE, NONE, NONE, NONE, NONE),
        (0, 34, 13, 23, 31, 41, 23, 49, 21),
        (0, 39, 120, 26, 34, 60, 49, 103, 66),
        (1, 25966, NONE, 74522, 76578, 30335, 220951, 15686, 1943),
        (1, NONE, NONE, NONE, NONE, 87886, 17228, 88143, 74265),
        (1, NONE, NONE, NONE, NONE, NONE, 89685, NONE, NONE),
        (0, 42, 15, NONE, NONE, 30, 30, 19, 28),
        (0, 108, 41, NONE, NONE, 49, 92, 37, 67),
        (1, 227633, 70667, 14658, 80176, 228918, 222750, 224549, 218381),
        (1, 138083, 1808, NONE, 24424, 9518, 11831, 30592, 23581),
        (1, 28279, NONE, NONE, NONE, 88143, 91227, 89428, 80176),
        (1, NONE, NONE, NONE, NONE, 134742, 136027, NONE, 131401),
        (0, 38, 23, 34, 61, 7, 7, 7, 128),
        (0, 112, 49, 108, 108, 88, 96, 117, 149),
        (1, 78192, 218895, 76578, 226862, NONE, NONE, NONE, NONE),
        (0, 62, NONE, NONE, NONE, 37, 34, 21, 68),
        (0, 85, NONE, NONE, NONE, 92, 38, 127, 81),
        (1, 71253, 71181, 224806, 11574, 15172, 24424, 32391, 3990),
        (1, 27765, 136541, 15172, 138340, 89428, 78377, 89685, 82232),
        (1, 221722, 3864, 142709, 87629, 223007, 224806, 220437, 219923),
        (1, 138340, NONE, 80176, NONE, NONE, NONE, NONE, 137055),
        (0, 9, 3, 18, 19, 9, 9, 9, 2),
        (0, 120, 128, 112, 112, 96, 119, 136, 136),
        (1, 80248, NONE, NONE, NONE, NONE, NONE, NONE, NONE),
        (0, 14, 12, 31, 30, 42, 42, 22, 33),
        (0, 55, 62, 42, 42, 53, 60, 53, 69),
        (1, 5663, 14915, 78634, 78634, 89685, 80433, 78377, 70667),
        (1, NONE, NONE, NONE, NONE, 5663, 14915, 13373, 6037),
        (0, 63, NONE, NONE, NONE, 29, 27, 28, 41),
        (0, 93, NONE, NONE, NONE, 35, 61, 126, 71),
        (1, 73309, 78377, 15429, 15172, 224806, 221979, 220694, 220180),
        (1, 223778, 220951, 90970, 87886, 78377, 15172, 26223, 90970),
        (1, 140653, 138340, 226862, 220951, 28022, 91484, 80433, 16642),
        (1, 7719, NONE, 140396, 140396, NONE, NONE, NONE, NONE),
        (0, 12, 20, 10, 7, 10, 10, 10, 3),
        (0, 128, 135, 120, 117, 104, 111, 144, 144),
        (1, 82304, NONE, NONE, NONE, NONE, NONE, NONE, NONE),
        (0, 57, 26, 49, 29, 57, 35, 29, 26),
        (0, 87, 38, 61, 43, 66, 45, 118, 87),
        (1, 7462, 15172, 72466, 78891, 7462, 76578, 72723, 94311),
        (1, 225834, 80433, 3607, 30078, 80433, 15429, 13630, 16899),
        (1, 140396, NONE, NONE, 68354, 222750, 226605, 222236, 218638),
        (0, 45, 34, 50, 37, 11, 11, 11, 4),
        (0, 97, 65, 62, 85, 135, 126, 88, 135),
        (1, 74337, 15429, 220951, 223007, NONE, NONE, NONE, NONE),
        (1, NONE, 70924, 5663, 91227, NONE, NONE, NONE, NONE),
        (1, NONE, 140653, 80433, 5663, NONE, NONE, NONE, NONE),
        (0, 10, 6, 12, 9, 65, 36, 23, 15),
        (0, 95, 119, 127, 127, 67, 52, 91, 59),
        (1, 13630, NONE, NONE, NONE, 13116, 78634, 91227, 88657),
        (1, NONE, NONE, NONE, NONE, 91484, 13116, 25966, 17156),
        (0, 11, 42, 22, 35, 15, 53, 31, 36),
        (0, 94, 66, 35, 66, 87, 57, 36, 111),
        (1, 231488, 72980, 13373, 91484, 224549, 224292, 222493, 221979),
        (1, 11831, 1551, 80690, 13373, 78634, 74779, 24167, 76321),
        (1, NONE, NONE, 223007, 222750, NONE, NONE, NONE, NONE),
        (0, 18, 9, 13, 10, NONE, NONE, 12, 5),
        (0, 105, 127, 135, 135, NONE, NONE, 119, 127),
        (1, 76393, NONE, NONE, NONE, 5406, 13373, NONE, 17413),
        (0, 13, 7, 30, 49, 18, 18, 66, 37),
        (0, 101, 50, 43, 67, 111, 103, 92, 60),
        (1, 13887, 3607, 13630, 72723, NONE, NONE, 91484, 78377),
        (1, 218638, 74522, 76835, 5406, NONE, NONE, 27765, 224806),
        (1, NONE, NONE, NONE, NONE, NONE, NONE, 224292, NONE),
        (0, 54, 35, 51, 15, 23, 65, 13, 6),
        (0, 113, 94, 65, 65, 93, 66, 102, 84),
        (1, 78449, 76578, 222750, 224549, 11317, 76835, NONE, 17670),
        (1, NONE, NONE, 3350, 27765, NONE, NONE, NONE, NONE),
        (0, 7, NONE, NONE, NONE, NONE, NONE, 34, 49),
        (0, 20, NONE, NONE, NONE, NONE, NONE, 67, 61),
        (1, 9261, 13630, 78891, 89685, 76835, 11060, 76578, 74522),
        (0, 22, 10, 19, 11, 19, 12, NONE, 22),
        (0, 92, 103, 126, 119, 119, 95, NONE, 119),
        (1, NONE, NONE, NONE, NONE, NONE, NONE, 30335, 220437),
        (0, 19, 43, 52, 86, 94, 88, 46, 7),
        (0, 121, 102, 67, 110, 95, 118, 57, 85),
        (1, 80505, 7462, 5406, 5149, 5149, 11317, 11317, 17927),
        (1, NONE, 78634, 80947, 76835, NONE, NONE, NONE, NONE),
        (0, 15, 18, 20, 12, 45, 37, 14, 57),
        (0, 50, 111, 111, 111, 100, 93, 109, 126),
        (1, NONE, NONE, NONE, NONE, NONE, NONE, NONE, 222236),
        (0, 46, 51, 7, 57, 12, 13, 65, 91),
        (0, 98, 101, 57, 87, 126, 102, 95, 97),
        (1, 74594, 80690, 81204, 7205, NONE, NONE, 30078, 15713),
        (0, 23, 57, 15, 59, 50, 59, 15, 30),
        (0, 58, 110, 86, 88, 59, 94, 93, 52),
        (1, NONE, 76835, NONE, NONE, NONE, NONE, NONE, NONE),
        (0, 21, 19, 21, 18, 27, 14, 20, 65),
        (0, 65, 87, 110, 118, 103, 110, 58, 102),
        (0, 30, 99, 58, 60, 58, 22, NONE, 92),
        (0, 106, 108, 87, 93, 117, 50, NONE, 98),
        (1, 76650, 78891, NONE, NONE, NONE, NONE, 28022, 13666),
        (0, 29, 14, 27, 20, 22, 58, 59, 34),
        (0, 66, 95, 118, 95, 101, 109, 99, 53),
        (0, 27, 22, 11, 14, 13, 15, 94, 1),
        (0, 114, 27, 59, 94, 110, 99, 60, 86),
        (1, 78706, 80947, NONE, NONE, NONE, NONE, NONE, NONE),
        (0, 35, 30, 60, 22, 43, 28, 112, 42),
        (0, 67, 58, 100, 50, 52, 29, 100, 101),
        (0, 43, 45, 37, 27, 14, 19, 51, 50),
        (0, 68, 29, 95, 103, 102, 117, 90, 94),
        (0, 28, 59, 6, 52, 21, 51, 42, 23),
        (0, 136, 21, 101, 58, 51, 100, 52, 99),
        (0, 51, 44, 45, 28, 36, 21, 101, 58),
        (0, 69, 53, 103, 102, 108, 101, 43, 108),
        (0, 37, 46, 14, 53, 109, 108, 50, 110),
        (0, 86, 52, 28, 101, 20, 43, 108, 35),
        (0, 59, 28, 53, 13, 44, 44, 35, 118),
        (0, 70, 54, 94, 51, 28, 20, 44, 43),
        (0, 44, 60, 36, 36, NONE, NONE, NONE, 44),
        (0, 61, 37, 102, 109, NONE, NONE, NONE, 93),
        (0, 36, 36, 29, 21, NONE, NONE, NONE, 51),
        (0, 52, 61, 44, 44, NONE, NONE, NONE, 117),
        (0, 53, NONE, NONE, NONE, NONE, NONE, NONE, 100),
        (0, 60, NONE, NONE, NONE, NONE, NONE, NONE, 109),
    ),
    (
        (1, 16200, 14144, 14144, 86344, 86344, 86344, 86344, 32576),
        (1, 67912, 86344, 86344, 16200, 16200, 16200, 16200, 86344),
        (1, 131144, 132429, 131915, 131658, 131144, 131144, 131144, 168504),
        (1, 69968, 16200, 16200, 14144, 12088, 14144, 12088, 34632),
        (1, 12088, 86601, 86601, 86601, 86601, 86601, 86601, 86601),
        (1, 131401, 131401, 131144, 131144, 131401, 131401, 131401, 169000),
        (1, 68169, 86858, 86858, 86858, 10032, 86858, 14144, 18184),
        (1, 14144, 18256, 17999, 18256, 86858, 18256, 71952, 69896),
        (1, 68683, 69896, 87372, 10032, 87115, 10032, 10032, 26408),
        (1, 17999, 12088, 18256, 87115, 17999, 69896, 69896, 86858),
        (1, 131658, 131658, 131401, 131401, 131658, 131658, 131658, 168752),
        (1, 68940, 87115, 12088, 12088, 18256, 12088, 86858, 28464),
        (1, 18256, 17999, 69896, 87372, 69896, 71952, 17999, 87115),
        (1, 131915, 132172, 131658, 131915, 131915, 131915, 131915, 168256),
        (1, 132172, 10032, 17742, 17742, 132172, 132172, 87115, 87372),
        (1, 7976, 131144, 10032, 17999, 71952, 17485, 132172, 87629),
        (1, 132429, 71952, 132172, 132172, 132429, 74008, 87372, 131144),
        (1, 68426, 74008, 132429, 132429, 7976, 132429, 132429, 87886),
        (1, 10032, NONE, 71952, NONE, 74008, 17742, 7976, 169744),
        (1, NONE, NONE, NONE, NONE, NONE, NONE, 87629, 71952),
        (0, 81, 63, 55, 55, 63, 63, 63, 9),
        (0, 127, 81, 81, 81, 81, 81, 81, 63),
        (1, 70225, 13887, 88657, 88657, 13887, 13887, 13887, 32319),
        (1, 30335, 88657, 11831, 11831, 88657, 88657, 88657, 74008),
        (1, 17228, 16971, 74008, 69896, 14144, 87115, 87886, 30520),
        (1, 69197, 76064, 133457, 132686, 132686, 17999, 22792, 169496),
        (1, 132686, NONE, NONE, NONE, NONE, 132686, 132686, NONE),
        (0, 82, 47, 63, 63, 55, 47, 55, 17),
        (0, 135, 82, 82, 82, 82, 82, 82, 47),
        (1, 70482, 88914, 88914, 88914, 11831, 9775, 11831, 28207),
        (1, 32391, 9775, 13887, 13887, 88914, 88914, 88914, 70153),
        (1, NONE, 131915, 87629, NONE, 132943, 132943, 132943, 169248),
        (0, 71, 55, 71, 70, 71, 25, 17, 10),
        (0, 83, 83, 83, 83, 83, 39, 71, 55),
        (1, 70739, 133971, 89171, 89171, 15943, 74265, 15943, 30263),
        (1, 17485, 11831, 15943, 15686, 89171, 7719, 74008, 72209),
        (1, NONE, NONE, NONE, 17485, 17228, 87372, NONE, NONE),
        (1, NONE, NONE, NONE, 71952, NONE, NONE, NONE, NONE),
        (0, 17, 70, 47, 71, 17, 17, 39, 12),
        (0, 103, 85, 84, 84, 39, 70, 83, 39),
        (1, 133457, 134485, 9775, 89428, 17485, 15686, 72209, 26151),
        (1, NONE, 17485, 89428, 15943, 76064, 87629, 133457, 131658),
        (1, NONE, 78120, 17485, 74008, 133457, 133457, NONE, NONE),
        (1, NONE, NONE, 133714, 7976, NONE, NONE, NONE, NONE),
        (1, NONE, NONE, NONE, 132943, NONE, NONE, NONE, NONE),
        (0, 84, 17, 70, 17, 25, 71, 47, 13),
        (0, 111, 71, 85, 47, 47, 83, 84, 70),
        (1, 17742, 17742, 87115, 9775, 17742, 15943, 9775, 76064),
        (1, 134228, 72209, 5920, 76064, 72209, 72209, 76064, 131915),
        (1, NONE, 132686, 134228, 133457, 133714, 133714, 133714, NONE),
        (0, 145, 136, 128, 104, 136, 112, 104, 88),
        (1, 86673, NONE, NONE, NONE, 32648, NONE, 24424, NONE),
        (0, 90, 90, 54, 69, 69, 54, 54, 18),
        (0, 126, 118, 90, 90, 90, 90, 85, 54),
        (1, 30078, 90970, 135770, 90970, 90970, 11574, 11574, 30006),
        (1, 72538, 28022, 11574, 15429, 74265, 90970, 78120, 72466),
        (1, 70996, 5920, 76064, 72209, 5920, 76064, 16971, 78120),
        (1, 3864, NONE, 7976, NONE, NONE, 26480, NONE, NONE),
        (0, 91, 91, 39, 39, 70, 46, 38, 19),
        (0, 110, 126, 91, 91, 91, 84, 86, 46),
        (2,),
        (1, 140910, 91227, 91227, 136027, 91227, 225320, 7462, 27950),
        (1, 233801, 30078, 229432, 223264, 231488, NONE, 223264, 219152),
        (1, NONE, 231488, NONE, NONE, NONE, NONE, NONE, NONE),
        (0, 0, 5, 3, 2, 0, 0, 0, 146),
        (1, 72795, 133457, 15686, 7719, 7719, 78120, 17228, 12178),
        (1, 5920, NONE, 78120, 133714, 133971, 9518, 89171, 70410),
        (1, NONE, NONE, 134485, NONE, NONE, 133971, 133971, 132172),
        (0, 146, 144, 136, 120, 127, 136, 96, 96),
        (1, 86930, NONE, NONE, NONE, NONE, NONE, NONE, NONE),
        (0, 25, 31, 38, 25, 33, 62, 68, 20),
        (0, 118, 92, 92, 46, 46, 85, 87, 62),
        (1, 28022, 136284, 7719, 74265, 9775, 32648, 17485, 70924),
        (1, 15943, 87372, 68611, 9518, 76321, 89171, 221208, 221208),
        (1, 234058, 7976, 231488, 227376, 229175, 231488, NONE, NONE),
        (1, NONE, 233544, NONE, NONE, NONE, NONE, NONE, NONE),
        (0, 1, 1, 0, 0, 1, 1, 1, 148),
        (1, 135770, 133714, 136027, 133971, 135770, 135770, 134228, 8084),
        (1, NONE, NONE, NONE, NONE, NONE, NONE, NONE, 132429),
        (0, 88, 88, 119, 128, 112, 135, 120, 104),
        (1, 72024, NONE, NONE, NONE, NONE, NONE, NONE, NONE),
        (0, 33, 25, 46, 33, 34, 31, 25, 11),
        (0, 102, 39, 93, 54, 54, 86, 69, 31),
        (1, NONE, 74265, 7462, 76321, 15429, 13630, 74265, 71181),
        (1, NONE, 15686, NONE, 78120, 76578, NONE, 17742, NONE),
        (1, NONE, 68097, NONE, NONE, NONE, NONE, NONE, NONE),
        (0, 41, 33, 17, 62, 61, 55, 33, 14),
        (0, 119, 67, 66, 92, 84, 87, 70, 89),
        (1, 219152, 76321, 72209, 13630, 225320, 231231, 76321, 15961),
        (1, NONE, 219152, 227119, 229432, NONE, NONE, 227376, 223264),
        (0, 2, 2, 1, 1, 2, 2, 2, 147),
        (1, 16714, 15943, 9518, 134228, 15686, 32391, 18256, 10131),
        (1, 145022, 135770, 136284, NONE, 87372, 134228, 134485, 72723),
        (1, NONE, NONE, NONE, NONE, 136027, NONE, NONE, 132686),
        (0, 144, 96, 144, 136, 120, 104, 128, 112),
        (1, 86416, NONE, NONE, NONE, NONE, NONE, NONE, NONE),
        (0, 99, 86, 99, 38, 62, 91, 18, 45),
        (0, 117, 117, 109, 99, 99, 127, 45, 82),
        (1, 142709, 27765, 16971, 7462, 93283, 80176, 72466, 27693),
        (1, 16971, 5663, 233544, 16971, 11574, 30335, 22368, 72980),
        (1, 233544, 80176, NONE, 231488, 227376, 223264, 229432, 22296),
        (1, NONE, 221208, NONE, NONE, NONE, NONE, NONE, 225320),
        (0, 3, 4, 2, 3, 3, 3, 3, 145),
        (1, 136027, 136027, 136541, 135770, 134228, 134485, 134742, 14225),
        (1, NONE, NONE, NONE, NONE, NONE, NONE, NONE, 132943),
        (0, 96, 104, 88, 144, 128, 120, 135, 90),
        (1, 74080, NONE, NONE, NONE, NONE, NONE, NONE, NONE),
        (0, 100, 68, 25, 45, 68, 33, 26, 27),
        (0, 109, 93, 117, 100, 85, 67, 30, 95),
        (1, 69454, 7719, 74265, 17228, 78120, 76321, 74522, 88914),
        (1, 1808, 68354, 17228, NONE, 13373, 5920, 15172, 24352),
        (1, NONE, NONE, NONE, NONE, NONE, 82232, NONE, NONE),
        (0, 47, 100, 33, 41, 31, 26, 27, 38),
        (1, 9775, NONE, NONE, NONE, NONE, NONE, NONE, NONE),
        (0, 49, 109, 68, 68, 86, 68, 61, 83),
        (1, 221208, 223264, 76321, 78377, 229432, 74522, 74779, 219666),
        (1, NONE, NONE, 219152, 233544, NONE, 227376, 231231, NONE),
        (0, 4, 0, 4, 4, 4, 4, 4, 0),
        (1, 74851, 16714, 3864, 3864, 82232, 7976, 28536, 16128),
        (1, 24167, 68868, 138083, 136284, 13630, 87886, 80176, 74779),
        (1, 142966, 134742, NONE, NONE, 138083, 134742, 134999, 24095),
        (1, NONE, NONE, NONE, NONE, NONE, NONE, NONE, 155974),
        (0, 104, 112, 96, 96, 118, 128, 111, 120),
        (1, 76136, NONE, NONE, NONE, NONE, NONE, NONE, NONE),
        (0, 31, 69, 41, 23, 26, 41, 41, 25),
        (0, 26, 84, 69, 26, 38, 69, 62, 29),
        (1, 75108, 89428, 78377, 74522, 74522, 16971, 82232, 89171),
        (1, 26223, 17228, 28279, 5920, 16971, 89428, 15429, 25894),
        (1, 223264, 69125, 221208, 221208, 87629, 229432, 225063, 227376),
        (1, NONE, 225320, NONE, NONE, 226862, NONE, NONE, NONE),
        (0, 5, 11, 5, 5, 5, 5, 5, 151),
        (0, 39, NONE, NONE, NONE, NONE, NONE, NONE, NONE),
        (1, 138854, 142709, 140653, 138083, 134485, 134999, NONE, 156222),
        (0, 89, 120, 104, 126, 144, 144, 110, 103),
        (1, 72281, NONE, NONE, NONE, NONE, NONE, NONE, NONE),
        (0, 34, 15, 23, 31, 41, 23, 49, 21),
        (0, NONE, 41, 26, 34, 60, 49, 103, 66),
        (1, 25966, 1808, 74522, 76578, 30335, 17228, 15686, 74265),
        (1, NONE, 70667, 14658, 80176, 87886, 89685, 88143, 1943),
        (0, 42, 23, NONE, NONE, 30, 30, 19, 28),
        (0, 108, 49, NONE, NONE, 49, 92, 37, 67),
        (1, 219409, 227376, NONE, 24424, 233544, 233544, 224806, 223007),
        (0, 6, 13, 34, 61, 6, 6, 6, 150),
        (1, 28279, 3864, NONE, NONE, 9518, 11831, 30592, 23581),
        (1, 138083, 136541, NONE, NONE, 88143, 91227, 89428, 80176),
        (0, 112, 128, 108, 108, NONE, NONE, NONE, NONE),
        (1, 78192, NONE, 76578, 228918, 134742, 136027, NONE, 131401),
        (0, 62, 12, NONE, NONE, 88, 96, 117, 128),
        (1, NONE, 70924, 223264, NONE, NONE, NONE, NONE, NONE),
        (0, 85, 62, 9, 6, 37, 34, 21, 68),
        (0, NONE, NONE, NONE, NONE, 92, 38, 127, 81),
        (1, 71253, 14915, 15172, 11574, 15172, 24424, 32391, 82232),
        (1, 27765, 78377, 80176, 87629, 89428, 78377, 89685, 3990),
        (1, 225320, 229432, 142709, 138340, 219152, 221208, 226605, 229432),
        (0, 38, 3, 112, 112, 7, 7, 7, 149),
        (0, 10, 38, 31, 30, NONE, NONE, NONE, NONE),
        (0, 55, NONE, 42, 42, NONE, NONE, NONE, NONE),
        (1, 138340, 138340, 78634, 78634, NONE, NONE, NONE, 137055),
        (0, 120, 135, NONE, NONE, 96, 119, 136, 136),
        (0, NONE, 26, NONE, NONE, 42, 42, 22, 33),
        (0, NONE, NONE, NONE, NONE, 53, 60, 53, 69),
        (1, 80248, 15172, 15429, 15172, 89685, 80433, 78377, 70667),
        (1, 5663, 80433, 90970, 87886, 5663, 14915, 13373, 6037),
        (0, 63, 34, NONE, NONE, 29, 27, 28, 41),
        (0, 93, 65, NONE, NONE, 35, 61, 126, 71),
        (1, 73309, 231231, 225320, 225320, 221208, 227119, 231488, 231488),
        (0, NONE, NONE, NONE, NONE, 9, 9, 9, 2),
        (1, 227376, NONE, NONE, NONE, 78377, 15172, 26223, 90970),
        (1, NONE, NONE, NONE, NONE, 28022, 91484, 80433, 16642),
        (0, 9, 20, 18, 19, 104, 111, 144, 144),
        (0, NONE, NONE, NONE, NONE, 57, 35, 29, 26),
        (0, NONE, NONE, NONE, NONE, 66, 45, 118, 87),
        (1, 7462, 15429, 140396, 140396, 7462, 76578, 72723, 94311),
        (1, 140653, 71181, NONE, NONE, 80433, 15429, 13630, 233544),
        (1, NONE, 140653, NONE, NONE, 223264, 225063, 233544, NONE),
        (0, 128, 119, 120, 117, 10, 10, 10, 3),
        (1, 82304, NONE, NONE, NONE, NONE, NONE, NONE, 16899),
        (0, 57, 42, 49, 29, 135, 126, 88, 135),
        (0, 87, 66, 61, 43, 65, 36, 23, 15),
        (1, 7719, 1551, 3607, 78891, NONE, NONE, NONE, NONE),
        (0, NONE, NONE, NONE, NONE, 67, 52, 91, 59),
        (1, 229432, 72980, 72466, 30078, 13116, 78634, 91227, 88657),
        (1, NONE, 227119, NONE, 68354, 91484, 13116, 25966, NONE),
        (0, 12, 6, 50, 37, 15, 53, 31, 36),
        (0, 11, 127, 62, 85, 87, 57, 36, 111),
        (1, 140396, NONE, 227376, 226605, 231231, 228918, 219152, 231231),
        (0, 97, 7, 10, 7, 11, 11, 11, 4),
        (1, 74337, NONE, 5663, 91227, 78634, 74779, 24167, 17156),
        (1, NONE, NONE, 80433, 5663, 5406, 13373, NONE, 76321),
        (0, 95, 50, 127, 127, 111, 103, 119, 127),
        (1, 13630, 3607, NONE, NONE, NONE, NONE, NONE, NONE),
        (0, 13, NONE, 22, 35, 23, 65, 66, 37),
        (0, 94, NONE, 35, 66, 93, 66, 92, 60),
        (1, 221465, 74522, 13373, 91484, 11317, 76835, 91484, 78377),
        (1, NONE, NONE, 80690, 13373, 76835, 11060, 27765, 229175),
        (1, NONE, NONE, 229175, 229175, 225063, 223007, NONE, NONE),
        (0, 45, 35, 12, 9, 18, 18, NONE, 5),
        (1, 9261, NONE, NONE, NONE, NONE, NONE, 227119, 17413),
        (0, 105, 94, 135, 135, 119, 95, 12, 84),
        (1, 76393, 229175, NONE, NONE, NONE, NONE, NONE, NONE),
        (0, 14, 9, 30, 49, 94, 88, 102, 49),
        (0, 101, NONE, 43, 67, 95, 118, 34, 61),
        (1, 11831, 76578, 13630, 5406, 5149, 11317, NONE, 74522),
        (1, 223521, 13630, 76835, 72723, NONE, NONE, NONE, NONE),
        (0, 18, 103, 51, 15, 45, 37, 67, 22),
        (0, 7, 43, 65, 65, 100, 93, NONE, 119),
        (0, 20, 102, NONE, NONE, NONE, NONE, NONE, NONE),
        (1, NONE, 78634, 231231, 231231, 227119, 220951, 76578, 218124),
        (0, 113, NONE, 13, 10, 19, 12, NONE, 6),
        (1, 78449, 7462, 3350, 27765, NONE, NONE, 30335, 17670),
        (1, 13887, 223007, 78891, 89685, NONE, NONE, NONE, NONE),
        (0, 21, 10, 126, 119, 126, 102, 46, 85),
        (0, 92, 111, 52, 86, 50, 59, 57, 57),
        (0, NONE, NONE, 67, 110, 59, 94, NONE, 126),
        (1, 225577, NONE, 5406, 5149, 228918, 222750, 222750, 218381),
        (1, NONE, NONE, 80947, 76835, NONE, NONE, NONE, NONE),
        (0, 54, 51, NONE, NONE, 12, 13, 13, 7),
        (0, 121, 101, NONE, NONE, NONE, NONE, NONE, NONE),
        (1, 80505, 80690, 228918, 227119, NONE, NONE, 11317, 17927),
        (0, 15, 57, 19, 11, 103, 110, 109, 91),
        (0, 50, 110, 111, 111, 58, 22, 65, 30),
        (1, 227633, 225063, NONE, NONE, NONE, NONE, NONE, NONE),
        (0, 19, 18, 7, 57, 117, 50, 95, 52),
        (0, 23, NONE, 57, 87, 22, 58, NONE, 65),
        (0, 98, NONE, NONE, NONE, 101, 109, NONE, 102),
        (1, 74594, 76835, 81204, 7205, 223007, 224806, 30078, 219923),
        (0, 58, 87, 15, 59, 27, 14, NONE, 97),
        (0, 22, 99, 86, 88, NONE, NONE, NONE, NONE),
        (0, 65, 108, NONE, NONE, NONE, NONE, NONE, NONE),
        (1, 221722, 78891, 225063, 225063, NONE, NONE, 224549, 15713),
        (0, 46, NONE, 20, 12, 110, 99, 14, 92),
        (0, 106, NONE, 110, 118, 43, 28, 93, 34),
        (1, 76650, 218895, NONE, NONE, NONE, NONE, NONE, NONE),
        (0, 29, 19, 58, 60, 52, 29, 20, 53),
        (0, 66, 22, 87, 93, NONE, NONE, NONE, NONE),
        (1, 223778, NONE, 224806, 226862, 224806, 221979, NONE, 220180),
        (0, 30, 27, 21, 18, 13, 15, 58, 98),
        (1, NONE, NONE, NONE, NONE, NONE, NONE, 28022, 13666),
        (0, 67, 95, 11, 95, 102, 117, 59, 86),
        (0, 114, NONE, 118, 14, 21, 51, 99, 42),
        (1, 78706, 80947, NONE, NONE, NONE, NONE, NONE, NONE),
        (0, 35, 29, 59, 94, 51, 100, NONE, 101),
        (0, 68, 58, 60, 22, 36, 21, NONE, 50),
        (0, 43, NONE, 100, 50, 108, 101, NONE, 94),
        (1, 225834, 220951, 226862, 220951, 222750, 226605, 220437, 218638),
        (0, 27, 14, 27, 20, 14, 19, 15, 1),
        (0, 136, 30, 95, 103, 109, 108, 94, 99),
        (0, 69, 59, 6, 52, 20, 43, 60, 58),
        (0, 51, 45, 101, 58, 44, 44, 112, 108),
        (1, 231488, NONE, 220951, 223007, 224549, 224292, 220694, 221979),
        (0, 28, 44, 37, 27, 28, 20, 100, 23),
        (0, 61, 53, 28, 102, NONE, NONE, 51, 110),
        (0, 86, 36, 103, 53, NONE, NONE, 90, 35),
        (0, 59, 52, 14, 101, NONE, NONE, 42, 118),
        (0, 53, 21, 53, 13, NONE, NONE, 52, 43),
        (0, 44, 46, 94, 51, NONE, NONE, NONE, 44),
        (1, 218638, NONE, 223007, 222750, NONE, NONE, 222236, 224806),
        (0, 37, 60, 45, 28, NONE, NONE, 101, 93),
        (0, 70, 28, 102, 109, NONE, NONE, 43, 51),
        (0, 52, 54, 29, 21, NONE, NONE, 50, 117),
        (0, 36, 61, 44, 44, NONE, NONE, NONE, NONE),
        (1, NONE, NONE, 222750, 224549, NONE, NONE, 222493, 220437),
        (0, 60, 37, 36, 36, NONE, NONE, 108, 100),
        (0, NONE, NONE, NONE, NONE, NONE, NONE, 35, 109),
        (0, NONE, NONE, NONE, NONE, NONE, NONE, 44, NONE),
        (1, NONE, NONE, NONE, NONE, NONE, NONE, 224292, 222236),
    ),
)
OWN = BAND * HALF


def device_of(row, cols):
    return row // cols, lax.rem(row, cols)


def kernel(cols_hbm, blocks_hbm, out_ref, cols_ref, blocks_ref, own, square, upper, flipped, in_sem, entered, send_sem, recv_sem):
    size = blocks_ref.shape[-1]
    loads = [
        pltpu.make_async_copy(cols_hbm, cols_ref, in_sem.at[0]),
        pltpu.make_async_copy(blocks_hbm, blocks_ref, in_sem.at[1]),
    ]
    for load in loads:
        load.start()
    cols = lax.axis_size("col")
    count = cols * lax.axis_size("row")
    me = lax.axis_index("row") * cols + lax.axis_index("col")
    place = lax.rem(me, RING)
    start = me - place
    targets = (
        start + lax.rem(place + 1, RING),
        start + lax.rem(place + RING - 1, RING),
        lax.rem(me + RING, count),
        lax.rem(me + count - RING, count),
    )
    barrier = pltpu.get_barrier_semaphore()
    peers = [device_of(target, cols) for target in targets]
    for peer in (peers[0], peers[1], peers[3]):
        pl.semaphore_signal(barrier, inc=1, device_id=peer, device_id_type=MESH)

    bits = [lax.rem(place // 2**n, 2) == 1 for n in range(3)]

    def pick(values):
        for bit in bits:
            values = [jnp.where(bit, high, low) for low, high in zip(values[::2], values[1::2])]
        return values[0]

    for load in loads:
        load.wait()
    missing = jnp.int32(0)
    for s in range(WINDOW - 1):
        offset = lax.rem(cols_ref[0, s] - me + BAND + count, count)
        missing += jnp.where(offset == s, 1, 0)

    for o in range(WINDOW):
        first = blocks_ref[0, min(o, WINDOW - 2)]
        second = blocks_ref[0, max(o - 1, 0)]
        block = jnp.where(o < missing, first, jnp.where(o == missing, jnp.zeros_like(first), second))
        own[:, o * size : (o + 1) * size] = block
        if o >= BAND:
            upper[OWN + o - BAND] = block
        else:
            slot = o * HALF + BAND - o
            upper[slot] = block.T
            flipped[slot] = block

    for d in range(HALF):
        flipped[OWN + d] = upper[OWN + d].T
    pl.semaphore_wait(barrier, 3)
    pl.semaphore_signal(entered, inc=1, device_id=peers[2], device_id_type=MESH)

    def copy(here, there, peer):
        return pltpu.make_async_remote_copy(
            src_ref=upper.at[here],
            dst_ref=upper.at[there],
            send_sem=send_sem,
            recv_sem=recv_sem.at[there],
            device_id=peer,
            device_id_type=MESH,
        )

    def send(code):
        direction = code >> 16
        ahead, far = (direction & 1) == 0, direction >= 2
        peer = tuple(
            jnp.where(far, jnp.where(ahead, c, d), jnp.where(ahead, a, b)) for a, b, c, d in zip(*peers)
        )
        copy(code & 255, (code >> 8) & 255, peer).start()

    def receive(here):
        copy(here, here, peers[0]).wait_recv()

    def turn(here):
        flipped[here] = upper[here].T

    def where_any(codes, code, action):
        if NONE in codes:
            pl.when(code != NONE)(functools.partial(action, code))
        else:
            action(code)

    def exchange(events):
        unturned, sending = [], False
        for kind, *codes in events:
            code = pick([jnp.int32(c) for c in codes]) if codes else None
            if kind == 1:
                where_any(codes, code, send)
            elif kind == 2:
                pl.semaphore_wait(entered, 1)
            else:
                if sending:
                    for late in unturned:
                        where_any(*late, turn)
                    unturned = []
                where_any(codes, code, receive)
                unturned.append((codes, code))
            sending = kind == 1
        for late in unturned:
            where_any(*late, turn)

    ring = lax.rem(me // RING, 16)
    ring = jnp.where((ring == 0) | (ring == 4), 1, 0)
    sends = jnp.int32(0)
    for n, events in enumerate(EVENTS):
        pl.when(ring == n)(functools.partial(exchange, events))
        counts = [sum(e[0] == 1 and e[1 + y] != NONE for e in events) for y in range(RING)]
        sends = jnp.where(ring == n, pick([jnp.int32(c) for c in counts]), sends)
    def block_at(k, j):
        if abs(k - j) > BAND:
            return jnp.zeros((size, size), upper.dtype)
        return upper[k * HALF + j - k] if k <= j else flipped[j * HALF + k - j]

    def product(factor, first, width):
        low, high = max(0, first - BAND), min(WINDOW, first + width + BAND)
        columns = [
            jnp.concatenate([block_at(k, j) for k in range(low, high)], axis=0) for j in range(first, first + width)
        ]
        return jnp.dot(
            factor[:, low * size : high * size],
            jnp.concatenate(columns, axis=1),
            preferred_element_type=jnp.float32,
        )

    for first in range(0, WINDOW, 2):
        width = min(2, WINDOW - first)
        total = product(own, first, width)
        for w in range(width):
            piece = total[:, w * size : (w + 1) * size]
            piece = jnp.where(missing == first + w, 0.0, piece).astype(square.dtype)
            square[:, (first + w) * size : (first + w + 1) * size] = piece
    for first in range(0, WINDOW, 2):
        width = min(2, WINDOW - first)
        total = product(square, first, width)
        for w in range(width):
            part = slice((first + w) * size, (first + w + 1) * size)
            value = 3.0 * square[:, part].astype(jnp.float32) - 2.0 * total[:, w * size : (w + 1) * size]
            value = value.astype(out_ref.dtype)
            s = first + w - 1
            if s >= 0:
                out_ref[0, s] = jnp.where(s < missing, before, value)
            before = value

    for number in sorted({sum(e[0] == 1 and e[1 + y] != NONE for e in events) for events in EVENTS for y in range(RING)}):
        blocks = upper.at[pl.ds(0, number)]
        pl.when(sends == number)(lambda blocks=blocks: pltpu.make_async_copy(blocks, blocks, send_sem).wait())


def per_device(block_cols, blocks):
    size = blocks.shape[-1]
    kind = blocks.dtype
    return pl.pallas_call(
        kernel,
        out_shape=jax.ShapeDtypeStruct(blocks.shape, kind),
        in_specs=[pl.BlockSpec(memory_space=pltpu.HBM)] * 2,
        out_specs=pl.BlockSpec(memory_space=pltpu.VMEM),
        scratch_shapes=[
            pltpu.SMEM(block_cols.shape, block_cols.dtype),
            pltpu.VMEM(blocks.shape, kind),
            pltpu.VMEM((size, WINDOW * size), kind),
            pltpu.VMEM((size, WINDOW * size), kind),
            pltpu.VMEM((WINDOW * HALF, size, size), kind),
            pltpu.VMEM((WINDOW * HALF, size, size), kind),
            pltpu.SemaphoreType.DMA((2,)),
            pltpu.SemaphoreType.REGULAR,
            pltpu.SemaphoreType.DMA,
            pltpu.SemaphoreType.DMA((WINDOW * HALF,)),
        ],
        compiler_params=pltpu.CompilerParams(collective_id=0, has_side_effects=True, vmem_limit_bytes=40 * 2**20),
        cost_estimate=pl.CostEstimate(flops=4 * 217 * size**3, bytes_accessed=2 * 2**20, transcendentals=0),
        name="purify",
    )(*(pltpu.with_memory_space_constraint(x, pltpu.HBM) for x in (block_cols, blocks)))


def solution(mesh):
    placed = (P(("row", "col"), None), P(("row", "col"), None, None, None))
    return jax.shard_map(
        per_device,
        mesh=mesh,
        in_specs=placed,
        out_specs=P(("row", "col"), None, None, None),
        check_vma=False,
    )
```
